512 devices in a mesh: ctx: 16 (over x, y), exp: 32 (over z, core).
Axes of the slice: x: 4, y: 4, z: 16, core: 2. Of those that a mesh axis runs over, the one named last changes fastest.
Arguments:
- residual: bfloat16 [32, 2048, 2048], P('exp', 'ctx'), may hold values from -12 to 12
- queries: bfloat16 [32, 2048, 1536], P('exp', 'ctx'), may hold values from -8 to 8
- latent: bfloat16 [32, 2048, 576], P('exp', 'ctx'), may hold values from -8 to 8
- key_up: bfloat16 [512, 1024], replicated, may hold values from -0.5 to 0.5
- value_up: bfloat16 [512, 1024], replicated, may hold values from -0.25 to 0.25
- out_proj: bfloat16 [1024, 2048], P(None, 'ctx'), may hold values from -0.1875 to 0.1875
- norm_gain: float32 [2048], replicated, may hold values from 0.4 to 2.5
- w_gate: bfloat16 [32, 2048, 704], P('exp', None, 'ctx'), may hold values from -0.125 to 0.125
- w_up: bfloat16 [32, 2048, 704], P('exp', None, 'ctx'), may hold values from -0.125 to 0.125
- w_down: bfloat16 [32, 704, 2048], P('exp', 'ctx'), may hold values from -0.21875 to 0.21875
- routes: int32 [32, 2048, 2], P('exp', 'ctx'), may hold values from 0 to 31, all different within a row; in each aligned block of 128 rows (0 to 127, 128 to 255, ..., all dimensions but the last counted through in order) at most 9 rows name the same one
- route_weights: float32 [32, 2048, 2], P('exp', 'ctx'), may hold values from 0.2 to 1
Outputs:
- layer_out: bfloat16 [32, 2048, 2048], P('exp', 'ctx')
The draws below stay inside these ranges and needn't reach their ends.
Inputs may be any that keep to these rules, and one draw needn't show every extreme that they name: `routes`: the 2 experts of a token differ; among the 128 tokens of one device (aligned blocks of the sequences laid end to end) no expert is named more than 9 times, a bound that some block reaches.
All inputs are finite; a program needn't handle non-finite values.
Results may differ from the reference program's by a relative error of at most 0.022.
Values may be sent and summed in bfloat16 or wider, within the bound.
No kernel may reach another device: no remote copies, remote signals or barrier semaphores. Data moves between devices by JAX's collectives and lax.ppermute only.
A program may use at most 128 MiB of HBM per device.

```python
import math
import jax
import jax.numpy as jnp
import numpy as np
from jax import lax

D = 2048
HEADS = 8
NOPE = 128
ROPE = 64
VHEAD = 128
LATENT = 512
FF = 704
TOPK = 2
TOK_DEV = 128
EXPERTS = 32
LEN = 2048
SEQS = 32
CAP = 9
N_CTX = 16


def draw_queries(key, part):
    key = jax.random.fold_in(key, 11)
    shape = (SEQS, LEN, HEADS * (NOPE + ROPE))
    values = jnp.clip(jax.random.normal(key, shape, jnp.float32), -6.0, 6.0)
    return values.astype(jnp.bfloat16)


def draw_latent(key, part):
    key = jax.random.fold_in(key, 23)
    shape = (SEQS, LEN, LATENT + ROPE)
    values = jnp.clip(jax.random.normal(key, shape, jnp.float32), -6.0, 6.0)
    return values.astype(jnp.bfloat16)


def draw_residual(key, part):
    key = jax.random.fold_in(key, 31)
    first, second, third = jax.random.split(key, 3)
    shape = (SEQS, LEN, D)
    row_scale = jnp.exp(jax.random.uniform(second, (SEQS, LEN, 1), jnp.float32, math.log(0.3), math.log(3.0)))
    col_scale = jnp.exp(jax.random.uniform(third, (D,), jnp.float32, math.log(0.3), math.log(3.0)))
    base = jax.random.normal(first, shape, jnp.float32)
    return jnp.clip(0.4 * base * row_scale * col_scale, -12.0, 12.0).astype(jnp.bfloat16)


def block_levels(own_key, shape, cuts, low, high):
    factor_of, own = 1.0, jax.random.fold_in(own_key, 6)
    for axis_at, blocks in cuts:
        heights = jnp.exp(jax.random.uniform(jax.random.fold_in(own, axis_at), (blocks,), jnp.float32, low / len(cuts), high / len(cuts)))
        factor_of = factor_of * jnp.repeat(heights, shape[axis_at] // blocks).reshape([-1 if axis == axis_at else 1 for axis in range(len(shape))])
    return factor_of


def shared_out(stream_key, own, number, rows, count, top, limit, lean):
    ranking = jax.random.permutation(stream_key, count)
    heavy_load, ordinary = portions_of(count, rows * top, limit, lean, True), portions_of(count, rows * top, limit, lean, False)
    places = jnp.arange(count)

    def named(tallies, offset_by):
        used = int((tallies > 0).sum())
        fixed = max(1, used // 4)
        moved = fixed + (places - fixed + offset_by * (used - fixed)) % max(1, count - fixed)
        return jnp.zeros((count,), jnp.int32).at[ranking[jnp.where(places < fixed, places, moved)]].set(jnp.asarray(tallies, jnp.int32))

    tallies = jnp.where(number % 4 == 0, named(heavy_load, number // 4), named(ordinary, number - number // 4 - 1))
    mixed = jax.random.permutation(jax.random.fold_in(own, 3), count)
    donor, sink = mixed[0:count // 2 * 2:2], mixed[1:count // 2 * 2:2]
    room = jnp.minimum(tallies[donor] - 1, limit - tallies[sink]) // 2
    room = jnp.where((donor == ranking[0]) | (sink == ranking[0]) | (tallies[sink] == 0), 0, jnp.maximum(room, 0))
    moved = jax.random.randint(jax.random.fold_in(own, 4), (count // 2,), 0, 1 << 20) % (room + 1)
    tallies = tallies.at[donor].add(-moved).at[sink].add(moved)
    items = jnp.searchsorted(jnp.cumsum(tallies), jnp.arange(rows * top), side="right").astype(jnp.int32)
    table = items.reshape(top, rows).T
    table = table[jax.random.permutation(jax.random.fold_in(own, 1), rows)]
    offset_by = jax.random.randint(jax.random.fold_in(own, 2), (rows, 1), 0, top)
    return jnp.take_along_axis(table, (jnp.arange(top)[None, :] + offset_by) % top, axis=1)


def portions_of(amount, total, most, skew, full):
    portions = [(1 << 20) // math.isqrt(grade ** skew) + 1 for grade in range(1, amount + 1)]
    largest = most if full else min(most, max(-(-total // amount), total * portions[0] // sum(portions)))
    least = 1 if total - largest >= amount - 1 else 0
    holding, spare = [largest] + [least] * (amount - 1), total - largest - least * (amount - 1)
    while spare > 0:
        movable = [i for i in range(1, amount) if holding[i] < largest] or [i for i in range(1, amount) if holding[i] < most]
        whole, left = sum([portions[i] for i in movable]), spare
        for i in movable:
            more = min(most - holding[i], max(1, left * portions[i] // whole), spare)
            holding[i] = holding[i] + more
            spare = spare - more
    return np.array(holding)


def noise(rng, dims, scale, limit, shards=(), kind=jnp.bfloat16):
    drawn = scale * jax.random.normal(rng, dims, jnp.float32)
    if shards:
        drawn = drawn * block_levels(rng, dims, shards, -0.22, 0.18)
    return jnp.clip(drawn, -limit, limit).astype(kind)


def setup_inputs(seed: int = 0) -> dict:
    streams_of = jax.random.split(jax.random.key(seed), 13)
    residual = draw_residual(jax.random.fold_in(streams_of[12], 71), 0)
    queries = draw_queries(jax.random.fold_in(streams_of[12], 71), 0)
    latent = draw_latent(jax.random.fold_in(streams_of[12], 71), 0)
    key_up = noise(streams_of[3], (LATENT, HEADS * NOPE), NOPE ** -0.5, 0.5)
    value_up = noise(streams_of[4], (LATENT, HEADS * VHEAD), LATENT ** -0.5, 0.25)
    out_proj = noise(streams_of[5], (HEADS * VHEAD, D), (HEADS * VHEAD) ** -0.5, 0.1875, ((1, 16),))
    norm_gain = jnp.clip(jnp.exp(jax.random.uniform(streams_of[6], (D,), jnp.float32, math.log(0.4), math.log(2.5))), 0.4, 2.5)
    w_gate = noise(streams_of[7], (EXPERTS, D, FF), D ** -0.5, 0.125, ((0, 32), (2, 16)))
    w_up = noise(streams_of[8], (EXPERTS, D, FF), D ** -0.5, 0.125, ((0, 32), (2, 16)))
    w_down = noise(streams_of[9], (EXPERTS, FF, D), FF ** -0.5, 0.21875, ((0, 32), (1, 16)))
    routes_keys = jax.random.split(jax.random.fold_in(streams_of[10], 1), SEQS * LEN // TOK_DEV)
    routes_turns = jax.random.permutation(jax.random.fold_in(streams_of[10], 3), SEQS * LEN // TOK_DEV)
    routes = jax.vmap(lambda own, number: shared_out(jax.random.fold_in(streams_of[10], 2), own, number, TOK_DEV, EXPERTS, TOPK, CAP, 2))(routes_keys, routes_turns).reshape((SEQS, LEN, TOPK))
    route_weights = jnp.clip(jnp.exp(math.log(1.0) - 1.609438 * jax.random.uniform(streams_of[11], (SEQS, LEN, TOPK), jnp.float32) ** block_levels(streams_of[11], (SEQS, LEN, TOPK), ((0, 32), (1, 16)), -0.2, 0.2)), 0.2, 1.0)
    return {"residual": residual, "queries": queries, "latent": latent, "key_up": key_up, "value_up": value_up, "out_proj": out_proj, "norm_gain": norm_gain, "w_gate": w_gate, "w_up": w_up, "w_down": w_down, "routes": routes, "route_weights": route_weights}


def attend_sequence(residual, queries, latent, key_up, value_up, out_proj):
    query_heads = queries.astype(jnp.float32).reshape(LEN, HEADS, NOPE + ROPE)
    key_heads = key_up.astype(jnp.float32).reshape(LATENT, HEADS, NOPE)
    absorbed = jnp.einsum('thn,lhn->thl', query_heads[:, :, :NOPE], key_heads).astype(jnp.bfloat16)
    latent_full = latent.astype(jnp.float32)
    scores = jnp.einsum('thl,ul->htu', absorbed.astype(jnp.float32), latent_full[:, :LATENT])
    scores = scores + jnp.einsum('thr,ur->htu', query_heads[:, :, NOPE:], latent_full[:, LATENT:])
    scores = scores * (NOPE + ROPE) ** (-0.5)
    positions = jnp.arange(LEN, dtype=jnp.int32)
    allowed = positions[None, :] <= positions[:, None]
    scores = jnp.where(allowed[None, :, :], scores, -1e+30)
    highest = lax.optimization_barrier(jnp.max(scores, axis=-1, keepdims=True))
    expo = jnp.exp(scores - highest)
    denominator = lax.optimization_barrier(jnp.sum(expo, axis=-1))
    probs = expo.astype(jnp.bfloat16)
    summed = jnp.einsum('htu,ul->thl', probs.astype(jnp.float32), latent_full[:, :LATENT])
    context = (summed / denominator.T[:, :, None]).astype(jnp.bfloat16)
    value_heads = value_up.astype(jnp.float32).reshape(LATENT, HEADS, VHEAD)
    values = jnp.einsum('thl,lhv->thv', context.astype(jnp.float32), value_heads).astype(jnp.bfloat16)
    values = values.reshape(LEN, HEADS * VHEAD)
    projected = jnp.dot(values, out_proj, preferred_element_type=jnp.float32)
    return (residual.astype(jnp.float32) + projected).astype(jnp.bfloat16)

def expert_rows(operands):
    slot_rows, gate_weight, up_weight, down_weight = operands
    gate_proj = jnp.dot(slot_rows, gate_weight, preferred_element_type=jnp.float32)
    up_proj = jnp.dot(slot_rows, up_weight, preferred_element_type=jnp.float32)
    activation = (jax.nn.silu(gate_proj) * up_proj).astype(jnp.bfloat16)
    return jnp.dot(activation, down_weight, preferred_element_type=jnp.float32).astype(jnp.bfloat16)

def mix_sequence(attended, norm_gain, w_gate, w_up, w_down, routes, route_weights):
    wide = attended.astype(jnp.float32)
    scale_rows = lax.rsqrt(lax.optimization_barrier(jnp.mean(wide * wide, axis=-1, keepdims=True)) + 1e-06)
    normed = (wide * scale_rows * norm_gain).astype(jnp.bfloat16)
    pairs = LEN * TOPK
    flat_routes = routes.reshape(pairs).astype(jnp.int32)
    onehot = (flat_routes[:, None] == jnp.arange(EXPERTS, dtype=jnp.int32)[None, :]).astype(jnp.int32)
    blocked = onehot.reshape(N_CTX, TOK_DEV * TOPK, EXPERTS)
    earlier = (jnp.cumsum(blocked, axis=1) - blocked).reshape(pairs, EXPERTS)
    position = lax.optimization_barrier(jnp.sum(earlier * onehot, axis=1))
    block_of = jnp.arange(pairs, dtype=jnp.int32) // (TOK_DEV * TOPK)
    token_of = (jnp.arange(pairs, dtype=jnp.int32) // TOPK).astype(jnp.int32)
    slot_index = ((flat_routes * N_CTX + block_of) * CAP + position).astype(jnp.int32)
    holder = jnp.zeros((EXPERTS * N_CTX * CAP, D), jnp.bfloat16).at[slot_index].set(normed[token_of])
    outputs = lax.map(expert_rows, (holder.reshape(EXPERTS, N_CTX * CAP, D), w_gate, w_up, w_down))
    picked = outputs.reshape(EXPERTS * N_CTX * CAP, D)[slot_index].astype(jnp.float32)
    picked = picked.reshape(LEN, TOPK, D)
    mixed = lax.optimization_barrier(jnp.sum(picked * route_weights.astype(jnp.float32)[:, :, None], axis=1))
    return (wide + mixed).astype(jnp.bfloat16)

def reference(residual, queries, latent, key_up, value_up, out_proj, norm_gain, w_gate, w_up, w_down, routes, route_weights):

    def one_sequence(operands):
        residual_seq, queries_seq, latent_seq, routes_seq, weights_seq = operands
        attended = attend_sequence(residual_seq, queries_seq, latent_seq, key_up, value_up, out_proj)
        return mix_sequence(attended, norm_gain, w_gate, w_up, w_down, routes_seq, weights_seq)
    return lax.map(one_sequence, (residual, queries, latent, routes, route_weights))
```

```python
import jax
import jax.numpy as jnp
from jax import lax
from jax.experimental import pallas as pl
from jax.experimental.pallas import tpu as pltpu
from jax.sharding import PartitionSpec as P

D = 2048
HEADS = 8
NOPE = 128
ROPE = 64
QK = NOPE + ROPE
VHEAD = 128
LATENT = 512
FF_DEV = 44
FF_PAD = 48
CAP = 9
LANES = 128
F32 = jnp.float32
BF16 = jnp.bfloat16
NT = (((1,), (1,)), ((), ()))
TN = (((0,), (0,)), ((), ()))
VMEM_LIMIT = 60 << 20


def call(kernel, out_shape, scratch=(), flops=0, moved=0, in_specs=None):
    options = {} if in_specs is None else {"in_specs": in_specs}
    return pl.pallas_call(
        kernel,
        out_shape=out_shape,
        scratch_shapes=list(scratch),
        compiler_params=pltpu.CompilerParams(vmem_limit_bytes=VMEM_LIMIT),
        cost_estimate=pl.CostEstimate(flops=flops, bytes_accessed=moved, transcendentals=0),
        **options,
    )


def vmem():
    return pl.BlockSpec(memory_space=pltpu.VMEM)


def slot_matrix(slots, k, rows):
    return lax.broadcasted_iota(jnp.int32, (rows, slots.shape[1]), 0) == slots[k : k + 1, :]


def fill_rows(matrix, source_ref, scratch, out_ref):
    rows = matrix.shape[0]
    parts = source_ref.shape[1] // LANES
    for j in range(0, parts, 2):
        chunk = jnp.dot(matrix, source_ref[:, j * LANES : (j + 2) * LANES], preferred_element_type=F32)
        scratch[pl.ds(j, rows, stride=parts), :] = chunk[:, :LANES]
        scratch[pl.ds(j + 1, rows, stride=parts), :] = chunk[:, LANES:]
    out_ref[...] = scratch[...].astype(BF16)


def pack_latent(latent_ref, out_ref):
    tokens = latent_ref.shape[0]
    half = tokens // 2
    for c in range(out_ref.shape[0]):
        for j in range(LATENT // LANES):
            out_ref[c, j * tokens : (j + 1) * tokens, :] = latent_ref[:, j * LANES : (j + 1) * LANES]
        start = LATENT // LANES * tokens
        rope = latent_ref[:, LATENT:]
        out_ref[c, start : start + half, :] = jnp.concatenate([rope[:half], rope[half:]], axis=1)


def dispatch_residual(routes_ref, residual_ref, out_ref, slots_ref, scratch):
    tokens = routes_ref.shape[1]
    rows = scratch.shape[0] * LANES // D
    expert = lax.broadcasted_iota(jnp.int32, (LANES, tokens), 0)
    first = (expert == routes_ref[0:1, :]).astype(F32)
    second = (expert == routes_ref[1:2, :]).astype(F32)
    row = lax.broadcasted_iota(jnp.int32, (tokens, tokens), 0)
    column = lax.broadcasted_iota(jnp.int32, (tokens, tokens), 1)
    before = (row < column).astype(BF16)
    count_first = jnp.dot(first.astype(BF16), before, preferred_element_type=F32)
    count_second = jnp.dot(second.astype(BF16), before, preferred_element_type=F32)
    count_second = count_second + jnp.sum(first, axis=1, keepdims=True)
    place_first = jnp.sum(count_first * first, axis=0, keepdims=True).astype(jnp.int32)
    place_second = jnp.sum(count_second * second, axis=0, keepdims=True).astype(jnp.int32)
    slots = jnp.concatenate(
        [routes_ref[0:1, :] * CAP + place_first, routes_ref[1:2, :] * CAP + place_second], axis=0
    )
    slots_ref[...] = slots
    matrix = (slot_matrix(slots, 0, rows) | slot_matrix(slots, 1, rows)).astype(BF16)
    fill_rows(matrix, residual_ref, scratch, out_ref)


def absorb(queries_ref, key_up_ref, out_ref):
    tokens = queries_ref.shape[0]
    for h in range(HEADS):
        query = queries_ref[:, h * QK : (h + 1) * QK]
        keys = key_up_ref[:, h * NOPE : (h + 1) * NOPE]
        out_ref[h * tokens : (h + 1) * tokens, :LATENT] = lax.dot_general(
            query[:, :NOPE], keys, NT, preferred_element_type=F32
        ).astype(BF16)
        out_ref[h * tokens : (h + 1) * tokens, LATENT:] = query[:, NOPE:]


def attend(place_ref, slots_ref, latent_ref, absorbed_ref, value_up_ref, values_ref, out_ref, keys, scratch):
    tokens = values_ref.shape[0]
    half = tokens // 2
    for c in range(latent_ref.shape[0]):
        for j in range(LATENT // LANES):
            keys[c * tokens : (c + 1) * tokens, j * LANES : (j + 1) * LANES] = latent_ref[
                c, j * tokens : (j + 1) * tokens, :
            ]
        rope = latent_ref[c, LATENT // LANES * tokens : LATENT // LANES * tokens + half, :]
        keys[c * tokens : c * tokens + half, LATENT:] = rope[:, :ROPE]
        keys[c * tokens + half : (c + 1) * tokens, LATENT:] = rope[:, ROPE:]
    span = keys.shape[0]
    group = 2 * tokens
    query_at = lax.broadcasted_iota(jnp.int32, (group, 1), 0) % tokens + place_ref[0] * tokens
    key_at = lax.broadcasted_iota(jnp.int32, (1, span), 1)
    allowed = key_at <= query_at
    for g in range(HEADS // 2):
        score = lax.dot_general(
            absorbed_ref[g * group : (g + 1) * group, :], keys[...], NT, preferred_element_type=F32
        )
        score = jnp.where(allowed, score * QK ** (-0.5), -1e30)
        highest = jnp.max(score, axis=1, keepdims=True)
        expo = jnp.exp(score - highest)
        denominator = jnp.sum(expo, axis=1, keepdims=True)
        context = jnp.dot(expo.astype(BF16), keys[:, :LATENT], preferred_element_type=F32)
        context = (context / denominator).astype(BF16)
        for i in range(2):
            h = 2 * g + i
            values_ref[:, h * VHEAD : (h + 1) * VHEAD] = jnp.dot(
                context[i * tokens : (i + 1) * tokens],
                value_up_ref[:, h * VHEAD : (h + 1) * VHEAD],
                preferred_element_type=F32,
            ).astype(BF16)
    rows = scratch.shape[0] * LANES // values_ref.shape[1]
    slots = slots_ref[...]
    matrix = (slot_matrix(slots, 0, rows) | slot_matrix(slots, 1, rows)).astype(BF16)
    fill_rows(matrix, values_ref, scratch, out_ref)


def lay_projection(parts, projection):
    depth = parts.shape[1]
    for c in range(parts.shape[0]):
        for j in range(parts.shape[2] // LANES):
            projection[j * depth : (j + 1) * depth, c * LANES : (c + 1) * LANES] = parts[
                c, :, j * LANES : (j + 1) * LANES
            ]


def take_rows(source_ref, scratch, parts, store):
    scratch[...] = source_ref[...].astype(F32)
    rows = scratch.shape[0] // parts
    for j in range(parts):
        store(j, scratch[pl.ds(j, rows, stride=parts), :])


def expert(
    residual_ref, values_ref, gain_ref, packed_ref, out_ref,
    parts, gate, up, down, projection, tall, short, values, wide, sems,
):
    depth = parts.shape[1]
    copies = []
    start = 0
    for n, buffer in enumerate((parts, gate, up, down)):
        size = buffer.shape[1]
        copies.append(pltpu.make_async_copy(packed_ref.at[:, start : start + size, :], buffer, sems.at[n]))
        copies[-1].start()
        start += size

    def keep_value(j, column):
        values[:, j * LANES : (j + 1) * LANES] = column.astype(BF16)

    def keep_wide(j, column):
        wide[:, j * LANES : (j + 1) * LANES] = column

    take_rows(values_ref, short, values.shape[1] // LANES, keep_value)
    take_rows(residual_ref, tall, D // LANES, keep_wide)
    copies[0].wait()
    lay_projection(parts, projection)
    attended = (wide[...] + jnp.dot(values[...], projection[...], preferred_element_type=F32)).astype(BF16)
    attended = attended.astype(F32)
    scale = lax.rsqrt(jnp.mean(attended * attended, axis=1, keepdims=True) + 1e-06)
    normed = (attended * scale * gain_ref[...]).astype(BF16)
    units = gate.shape[0] * gate.shape[1]
    copies[1].wait()
    gate_proj = lax.dot_general(normed, gate[...].reshape(units, D), NT, preferred_element_type=F32)
    copies[2].wait()
    up_proj = lax.dot_general(normed, up[...].reshape(units, D), NT, preferred_element_type=F32)
    activation = (gate_proj / (1.0 + jnp.exp(-gate_proj)) * up_proj).astype(BF16)
    copies[3].wait()
    rows = activation.shape[0]
    down_all = down[...].reshape(units, D)
    for j in range(0, D // LANES, 2):
        chunk = jnp.dot(activation, down_all[:, j * LANES : (j + 2) * LANES], preferred_element_type=F32)
        tall[pl.ds(j, rows, stride=D // LANES), :] = chunk[:, :LANES]
        tall[pl.ds(j + 1, rows, stride=D // LANES), :] = chunk[:, LANES:]
    out_ref[...] = tall[...].astype(BF16)


def home(residual_ref, values_ref, packed_ref, out_ref, parts, projection, sem):
    copy = pltpu.make_async_copy(packed_ref.at[:, : parts.shape[1], :], parts, sem)
    copy.start()
    copy.wait()
    lay_projection(parts, projection)
    projected = jnp.dot(values_ref[...], projection[...], preferred_element_type=F32)
    out_ref[...] = (residual_ref[...].astype(F32) + projected).astype(BF16)


def combine(slots_ref, weights_ref, attended_ref, rows_ref, out_ref, tall):
    slots = slots_ref[...]
    rows = tall.shape[0] * LANES // D
    first = slot_matrix(slots, 0, rows).astype(BF16)
    second = slot_matrix(slots, 1, rows).astype(BF16)
    weight_first = weights_ref[:, 0:1]
    weight_second = weights_ref[:, 1:2]

    def add(j, column):
        column = column.astype(BF16)
        picked_first = lax.dot_general(first, column, TN, preferred_element_type=F32)
        picked_second = lax.dot_general(second, column, TN, preferred_element_type=F32)
        mixed = picked_first * weight_first + picked_second * weight_second
        at = slice(j * LANES, (j + 1) * LANES)
        out_ref[:, at] = (attended_ref[:, at].astype(F32) + mixed).astype(BF16)

    take_rows(rows_ref, tall, D // LANES, add)


def body(
    residual, queries, latent, key_up, value_up, out_proj, norm_gain,
    w_gate, w_up, w_down, routes, route_weights,
):
    tokens = residual.shape[1]
    n_ctx = lax.axis_size("ctx")
    n_exp = lax.axis_size("exp")
    rows = n_exp * CAP
    flat = values_width = HEADS * VHEAD
    tall_rows = rows * D // LANES
    short_rows = rows * values_width // LANES
    block_rows = tokens * (LATENT + ROPE) // LANES

    latent_out = call(
        pack_latent, jax.ShapeDtypeStruct((n_ctx, block_rows, LANES), BF16), moved=3 << 20
    )(latent[0])
    latent_all = lax.all_to_all(latent_out, "ctx", split_axis=0, concat_axis=0, tiled=True)

    residual_out, slots = call(
        dispatch_residual,
        [jax.ShapeDtypeStruct((tall_rows, LANES), BF16), jax.ShapeDtypeStruct((2, tokens), jnp.int32)],
        scratch=[pltpu.VMEM((tall_rows, LANES), F32)],
        flops=2 * rows * tokens * D,
        moved=3 << 20,
    )(routes[0].T, residual[0])
    residual_rows = lax.all_to_all(
        residual_out.reshape(n_exp, tall_rows // n_exp, LANES), "exp", split_axis=0, concat_axis=0, tiled=True
    )

    pad = ((0, FF_PAD - w_gate.shape[2]), (0, 0))
    depth = flat // n_ctx
    packed = jnp.concatenate(
        [
            out_proj.reshape(n_ctx, depth, LANES).transpose(1, 0, 2).reshape(depth, n_ctx * LANES),
            jnp.pad(w_gate[0].T, pad),
            jnp.pad(w_up[0].T, pad),
            jnp.pad(w_down[0], pad),
        ],
        axis=0,
    )
    packed_all = lax.all_gather(packed, "ctx")

    absorbed = call(
        absorb,
        jax.ShapeDtypeStruct((HEADS * tokens, LATENT + ROPE), BF16),
        flops=2 * tokens * HEADS * NOPE * LATENT,
        moved=3 << 20,
    )(queries[0], key_up)
    place = lax.axis_index("ctx").astype(jnp.int32).reshape(1)
    values, values_out = call(
        attend,
        [
            jax.ShapeDtypeStruct((tokens, values_width), BF16),
            jax.ShapeDtypeStruct((short_rows, LANES), BF16),
        ],
        scratch=[
            pltpu.VMEM((n_ctx * tokens, LATENT + ROPE), BF16),
            pltpu.VMEM((short_rows, LANES), F32),
        ],
        flops=4 << 30,
        moved=6 << 20,
        in_specs=[pl.BlockSpec(memory_space=pltpu.SMEM)] + [vmem()] * 4,
    )(place, slots, latent_all, absorbed, value_up)
    values_rows = lax.all_to_all(
        values_out.reshape(n_exp, short_rows // n_exp, LANES), "exp", split_axis=0, concat_axis=0, tiled=True
    )

    weights_shape = (n_ctx, FF_PAD, D)
    result = call(
        expert,
        jax.ShapeDtypeStruct((tall_rows, LANES), BF16),
        scratch=[
            pltpu.VMEM((n_ctx, depth, D), BF16),
            pltpu.VMEM(weights_shape, BF16),
            pltpu.VMEM(weights_shape, BF16),
            pltpu.VMEM(weights_shape, BF16),
            pltpu.VMEM((values_width, D), BF16),
            pltpu.VMEM((tall_rows, LANES), F32),
            pltpu.VMEM((short_rows, LANES), F32),
            pltpu.VMEM((rows, values_width), BF16),
            pltpu.VMEM((rows, D), F32),
            pltpu.SemaphoreType.DMA((4,)),
        ],
        flops=4 << 30,
        moved=16 << 20,
        in_specs=[vmem()] * 3 + [pl.BlockSpec(memory_space=pl.ANY)],
    )(
        residual_rows.reshape(tall_rows, LANES),
        values_rows.reshape(short_rows, LANES),
        norm_gain.reshape(1, D),
        packed_all,
    )
    returned = lax.all_to_all(
        result.reshape(n_exp, tall_rows // n_exp, LANES), "exp", split_axis=0, concat_axis=0, tiled=True
    )

    attended = call(
        home,
        jax.ShapeDtypeStruct((tokens, D), BF16),
        scratch=[
            pltpu.VMEM((n_ctx, depth, D), BF16),
            pltpu.VMEM((values_width, D), BF16),
            pltpu.SemaphoreType.DMA,
        ],
        flops=2 * tokens * D * values_width,
        moved=6 << 20,
        in_specs=[vmem()] * 2 + [pl.BlockSpec(memory_space=pl.ANY)],
    )(residual[0], values, packed_all)
    layer_out = call(
        combine,
        jax.ShapeDtypeStruct((tokens, D), BF16),
        scratch=[pltpu.VMEM((tall_rows, LANES), F32)],
        flops=4 * rows * tokens * D,
        moved=3 << 20,
    )(slots, route_weights[0], attended, returned.reshape(tall_rows, LANES))
    return layer_out[None]


def solution(mesh):
    return jax.shard_map(
        body,
        mesh=mesh,
        in_specs=(
            P("exp", "ctx", None),
            P("exp", "ctx", None),
            P("exp", "ctx", None),
            P(),
            P(),
            P(None, "ctx"),
            P(),
            P("exp", None, "ctx"),
            P("exp", None, "ctx"),
            P("exp", "ctx", None),
            P("exp", "ctx", None),
            P("exp", "ctx", None),
        ),
        out_specs=P("exp", "ctx", None),
        check_vma=False,
    )
```

```python
import jax
import jax.numpy as jnp
from jax import lax
from jax.experimental import pallas as pl
from jax.experimental.pallas import tpu as pltpu
from jax.sharding import PartitionSpec as P

D = 2048
HEADS = 8
NOPE = 128
ROPE = 64
QK = NOPE + ROPE
VHEAD = 128
LATENT = 512
FF_DEV = 44
FF_PAD = 48
CAP = 9
LANES = 128
F32 = jnp.float32
BF16 = jnp.bfloat16
NT = (((1,), (1,)), ((), ()))
TN = (((0,), (0,)), ((), ()))
VMEM_LIMIT = 60 << 20


def call(kernel, out_shape, scratch=(), flops=0, moved=0, in_specs=None):
    options = {} if in_specs is None else {"in_specs": in_specs}
    return pl.pallas_call(
        kernel,
        out_shape=out_shape,
        scratch_shapes=list(scratch),
        compiler_params=pltpu.CompilerParams(vmem_limit_bytes=VMEM_LIMIT),
        cost_estimate=pl.CostEstimate(flops=flops, bytes_accessed=moved, transcendentals=0),
        **options,
    )


def vmem():
    return pl.BlockSpec(memory_space=pltpu.VMEM)


def slot_matrix(slots, k, rows):
    return lax.broadcasted_iota(jnp.int32, (rows, slots.shape[1]), 0) == slots[k : k + 1, :]


def fill_rows(matrix, source_ref, scratch, out_ref):
    rows = matrix.shape[0]
    parts = source_ref.shape[1] // LANES
    for j in range(0, parts, 2):
        chunk = jnp.dot(matrix, source_ref[:, j * LANES : (j + 2) * LANES], preferred_element_type=F32)
        scratch[pl.ds(j, rows, stride=parts), :] = chunk[:, :LANES]
        scratch[pl.ds(j + 1, rows, stride=parts), :] = chunk[:, LANES:]
    out_ref[...] = scratch[...].astype(BF16)


def pack_latent(latent_ref, out_ref):
    tokens = latent_ref.shape[0]
    half = tokens // 2
    for j in range(LATENT // LANES):
        out_ref[j * tokens : (j + 1) * tokens, :] = latent_ref[:, j * LANES : (j + 1) * LANES]
    rope = latent_ref[:, LATENT:]
    out_ref[LATENT // LANES * tokens :, :] = jnp.concatenate([rope[:half], rope[half:]], axis=1)


def dispatch_residual(routes_ref, residual_ref, out_ref, slots_ref, scratch):
    tokens = routes_ref.shape[1]
    rows = scratch.shape[0] * LANES // D
    expert = lax.broadcasted_iota(jnp.int32, (LANES, tokens), 0)
    first = (expert == routes_ref[0:1, :]).astype(F32)
    second = (expert == routes_ref[1:2, :]).astype(F32)
    row = lax.broadcasted_iota(jnp.int32, (tokens, tokens), 0)
    column = lax.broadcasted_iota(jnp.int32, (tokens, tokens), 1)
    before = (row < column).astype(BF16)
    count_first = jnp.dot(first.astype(BF16), before, preferred_element_type=F32)
    count_second = jnp.dot(second.astype(BF16), before, preferred_element_type=F32)
    count_second = count_second + jnp.sum(first, axis=1, keepdims=True)
    place_first = jnp.sum(count_first * first, axis=0, keepdims=True).astype(jnp.int32)
    place_second = jnp.sum(count_second * second, axis=0, keepdims=True).astype(jnp.int32)
    slots = jnp.concatenate(
        [routes_ref[0:1, :] * CAP + place_first, routes_ref[1:2, :] * CAP + place_second], axis=0
    )
    slots_ref[...] = slots
    matrix = (slot_matrix(slots, 0, rows) | slot_matrix(slots, 1, rows)).astype(BF16)
    fill_rows(matrix, residual_ref, scratch, out_ref)


def absorb(queries_ref, key_up_ref, out_ref):
    tokens = queries_ref.shape[0]
    for h in range(HEADS):
        query = queries_ref[:, h * QK : (h + 1) * QK]
        keys = key_up_ref[:, h * NOPE : (h + 1) * NOPE]
        out_ref[h * tokens : (h + 1) * tokens, :LATENT] = lax.dot_general(
            query[:, :NOPE], keys, NT, preferred_element_type=F32
        ).astype(BF16)
        out_ref[h * tokens : (h + 1) * tokens, LATENT:] = query[:, NOPE:]


def lay_keys(blocks, first, keys, tokens):
    half = tokens // 2
    for b in range(blocks.shape[0]):
        at = (first + b) * tokens
        for j in range(LATENT // LANES):
            keys[at : at + tokens, j * LANES : (j + 1) * LANES] = blocks[b, j * tokens : (j + 1) * tokens, :]
        rope = blocks[b, LATENT // LANES * tokens :, :]
        keys[at : at + half, LATENT:] = rope[:, :ROPE]
        keys[at + half : at + tokens, LATENT:] = rope[:, ROPE:]


def scores(absorbed_ref, keys, key_at, place, g, tokens):
    group = 2 * tokens
    query_at = lax.broadcasted_iota(jnp.int32, (group, 1), 0) % tokens + place * tokens
    score = lax.dot_general(
        absorbed_ref[g * group : (g + 1) * group, :], keys[...], NT, preferred_element_type=F32
    )
    return jnp.where(key_at <= query_at, score * QK ** (-0.5), -1e30)


def attend_near(place_ref, key_at_ref, near_ref, up_ref, down_ref, absorbed_ref, sum_ref, highest_ref, denominator_ref, keys):
    group = absorbed_ref.shape[0] // (HEADS // 2)
    tokens = group // 2
    blocks = near_ref.shape[0]
    for n, ref in enumerate((near_ref, up_ref, down_ref)):
        lay_keys(ref, n * blocks, keys, tokens)
    for g in range(HEADS // 2):
        at = slice(g * group, (g + 1) * group)
        score = scores(absorbed_ref, keys, key_at_ref[...], place_ref[0], g, tokens)
        highest = jnp.max(score, axis=1, keepdims=True)
        expo = jnp.exp(score - highest)
        highest_ref[at, :] = highest
        denominator_ref[at, :] = jnp.sum(expo, axis=1, keepdims=True)
        sum_ref[at, :] = jnp.dot(expo.astype(BF16), keys[:, :LATENT], preferred_element_type=F32)


def attend_far(
    place_ref, slots_ref, key_at_ref, first_ref, second_ref, absorbed_ref, sum_ref, highest_ref, denominator_ref,
    value_up_ref, values_ref, out_ref, keys, scratch,
):
    tokens = values_ref.shape[0]
    group = 2 * tokens
    lay_keys(first_ref, 0, keys, tokens)
    lay_keys(second_ref, first_ref.shape[0], keys, tokens)
    for g in range(HEADS // 2):
        at = slice(g * group, (g + 1) * group)
        score = scores(absorbed_ref, keys, key_at_ref[...], place_ref[0], g, tokens)
        before = highest_ref[at, :]
        highest = jnp.maximum(before, jnp.max(score, axis=1, keepdims=True))
        factor = jnp.exp(before - highest)
        expo = jnp.exp(score - highest)
        denominator = denominator_ref[at, :] * factor + jnp.sum(expo, axis=1, keepdims=True)
        context = jnp.dot(expo.astype(BF16), keys[:, :LATENT], preferred_element_type=F32)
        context = ((context + sum_ref[at, :] * factor) / denominator).astype(BF16)
        for i in range(2):
            h = 2 * g + i
            values_ref[:, h * VHEAD : (h + 1) * VHEAD] = jnp.dot(
                context[i * tokens : (i + 1) * tokens],
                value_up_ref[:, h * VHEAD : (h + 1) * VHEAD],
                preferred_element_type=F32,
            ).astype(BF16)
    rows = scratch.shape[0] * LANES // values_ref.shape[1]
    slots = slots_ref[...]
    matrix = (slot_matrix(slots, 0, rows) | slot_matrix(slots, 1, rows)).astype(BF16)
    fill_rows(matrix, values_ref, scratch, out_ref)


def lay_projection(parts, projection):
    depth = parts.shape[1]
    for c in range(parts.shape[0]):
        for j in range(parts.shape[2] // LANES):
            projection[j * depth : (j + 1) * depth, c * LANES : (c + 1) * LANES] = parts[
                c, :, j * LANES : (j + 1) * LANES
            ]


def take_rows(source_ref, scratch, parts, store):
    scratch[...] = source_ref[...].astype(F32)
    rows = scratch.shape[0] // parts
    for j in range(parts):
        store(j, scratch[pl.ds(j, rows, stride=parts), :])


def expert(
    residual_ref, values_ref, gain_ref, packed_ref, out_ref,
    parts, gate, up, down, projection, tall, short, values, wide, sems,
):
    depth = parts.shape[1]
    copies = []
    start = 0
    for n, buffer in enumerate((parts, gate, up, down)):
        size = buffer.shape[1]
        copies.append(pltpu.make_async_copy(packed_ref.at[:, start : start + size, :], buffer, sems.at[n]))
        copies[-1].start()
        start += size

    def keep_value(j, column):
        values[:, j * LANES : (j + 1) * LANES] = column.astype(BF16)

    def keep_wide(j, column):
        wide[:, j * LANES : (j + 1) * LANES] = column

    take_rows(values_ref, short, values.shape[1] // LANES, keep_value)
    take_rows(residual_ref, tall, D // LANES, keep_wide)
    copies[0].wait()
    lay_projection(parts, projection)
    attended = (wide[...] + jnp.dot(values[...], projection[...], preferred_element_type=F32)).astype(BF16)
    attended = attended.astype(F32)
    scale = lax.rsqrt(jnp.mean(attended * attended, axis=1, keepdims=True) + 1e-06)
    normed = (attended * scale * gain_ref[...]).astype(BF16)
    units = gate.shape[0] * gate.shape[1]
    copies[1].wait()
    gate_proj = lax.dot_general(normed, gate[...].reshape(units, D), NT, preferred_element_type=F32)
    copies[2].wait()
    up_proj = lax.dot_general(normed, up[...].reshape(units, D), NT, preferred_element_type=F32)
    activation = (gate_proj / (1.0 + jnp.exp(-gate_proj)) * up_proj).astype(BF16)
    copies[3].wait()
    rows = activation.shape[0]
    down_all = down[...].reshape(units, D)
    for j in range(0, D // LANES, 2):
        chunk = jnp.dot(activation, down_all[:, j * LANES : (j + 2) * LANES], preferred_element_type=F32)
        tall[pl.ds(j, rows, stride=D // LANES), :] = chunk[:, :LANES]
        tall[pl.ds(j + 1, rows, stride=D // LANES), :] = chunk[:, LANES:]
    out_ref[...] = tall[...].astype(BF16)


def home(residual_ref, values_ref, packed_ref, out_ref, parts, projection, sem):
    copy = pltpu.make_async_copy(packed_ref.at[:, : parts.shape[1], :], parts, sem)
    copy.start()
    copy.wait()
    lay_projection(parts, projection)
    projected = jnp.dot(values_ref[...], projection[...], preferred_element_type=F32)
    out_ref[...] = (residual_ref[...].astype(F32) + projected).astype(BF16)


def combine(slots_ref, weights_ref, attended_ref, rows_ref, out_ref, tall):
    slots = slots_ref[...]
    rows = tall.shape[0] * LANES // D
    first = slot_matrix(slots, 0, rows).astype(BF16)
    second = slot_matrix(slots, 1, rows).astype(BF16)
    weight_first = weights_ref[:, 0:1]
    weight_second = weights_ref[:, 1:2]

    def add(j, column):
        column = column.astype(BF16)
        picked_first = lax.dot_general(first, column, TN, preferred_element_type=F32)
        picked_second = lax.dot_general(second, column, TN, preferred_element_type=F32)
        mixed = picked_first * weight_first + picked_second * weight_second
        at = slice(j * LANES, (j + 1) * LANES)
        out_ref[:, at] = (attended_ref[:, at].astype(F32) + mixed).astype(BF16)

    take_rows(rows_ref, tall, D // LANES, add)


def body(
    residual, queries, latent, key_up, value_up, out_proj, norm_gain,
    w_gate, w_up, w_down, routes, route_weights,
):
    tokens = residual.shape[1]
    n_ctx = lax.axis_size("ctx")
    n_exp = lax.axis_size("exp")
    rows = n_exp * CAP
    flat = values_width = HEADS * VHEAD
    tall_rows = rows * D // LANES
    short_rows = rows * values_width // LANES
    block_rows = tokens * (LATENT + ROPE) // LANES

    residual_out, slots = call(
        dispatch_residual,
        [jax.ShapeDtypeStruct((tall_rows, LANES), BF16), jax.ShapeDtypeStruct((2, tokens), jnp.int32)],
        scratch=[pltpu.VMEM((tall_rows, LANES), F32)],
        flops=2 * rows * tokens * D,
        moved=3 << 20,
    )(routes[0].T, residual[0])
    residual_rows = lax.all_to_all(
        residual_out.reshape(n_exp, tall_rows // n_exp, LANES), "exp", split_axis=0, concat_axis=0, tiled=True
    )

    pad = ((0, FF_PAD - w_gate.shape[2]), (0, 0))
    depth = flat // n_ctx
    packed = jnp.concatenate(
        [
            out_proj.reshape(n_ctx, depth, LANES).transpose(1, 0, 2).reshape(depth, n_ctx * LANES),
            jnp.pad(w_gate[0].T, pad),
            jnp.pad(w_up[0].T, pad),
            jnp.pad(w_down[0], pad),
        ],
        axis=0,
    )
    packed_all = lax.all_gather(packed, "ctx")

    mine, residual_out = lax.optimization_barrier((latent[0], residual_out))
    block = call(pack_latent, jax.ShapeDtypeStruct((block_rows, LANES), BF16))(mine)
    side = 4

    def shift(array, along_x, along_y):
        pairs = [
            (x * side + y, (x + along_x) % side * side + (y + along_y) % side)
            for x in range(side)
            for y in range(side)
        ]
        return lax.ppermute(array, "ctx", pairs)

    near = jnp.stack([block, shift(block, 0, 1), shift(block, 0, -1), shift(block, 0, 2)])
    up = shift(near, 1, 0)
    down = shift(near, -1, 0)
    far_up = shift(up[:2], 1, 0)
    far_down = shift(down[2:], -1, 0)
    here = lax.axis_index("ctx").astype(jnp.int32)
    offsets = [(0, 0), (0, -1), (0, 1), (0, -2)]
    offsets = [(dx, dy) for dx in (0, -1, 1, -2) for _, dy in offsets]
    owner = jnp.stack(
        [(here // side + dx + side) % side * side + (here % side + dy + side) % side for dx, dy in offsets]
    )
    key_at = (owner[:, None] * tokens + jnp.arange(tokens, dtype=jnp.int32)[None, :]).reshape(1, n_ctx * tokens)
    split = 3 * side * tokens

    absorbed = call(
        absorb,
        jax.ShapeDtypeStruct((HEADS * tokens, LATENT + ROPE), BF16),
        flops=2 * tokens * HEADS * NOPE * LATENT,
        moved=3 << 20,
    )(queries[0], key_up)
    place = here.reshape(1)
    smem = pl.BlockSpec(memory_space=pltpu.SMEM)
    column = jax.ShapeDtypeStruct((HEADS * tokens, 1), F32)
    summed, highest, denominator = call(
        attend_near,
        [jax.ShapeDtypeStruct((HEADS * tokens, LATENT), F32), column, column],
        scratch=[pltpu.VMEM((split, LATENT + ROPE), BF16)],
        flops=3 << 30,
        moved=6 << 20,
        in_specs=[smem] + [vmem()] * 5,
    )(place, key_at[:, :split], near, up, down, absorbed)
    values, values_out = call(
        attend_far,
        [
            jax.ShapeDtypeStruct((tokens, values_width), BF16),
            jax.ShapeDtypeStruct((short_rows, LANES), BF16),
        ],
        scratch=[
            pltpu.VMEM((side * tokens, LATENT + ROPE), BF16),
            pltpu.VMEM((short_rows, LANES), F32),
        ],
        flops=1 << 30,
        moved=6 << 20,
        in_specs=[smem] + [vmem()] * 9,
    )(place, slots, key_at[:, split:], far_up, far_down, absorbed, summed, highest, denominator, value_up)
    values_out, residual_rows = lax.optimization_barrier((values_out, residual_rows))
    values_rows = lax.all_to_all(
        values_out.reshape(n_exp, short_rows // n_exp, LANES), "exp", split_axis=0, concat_axis=0, tiled=True
    )

    weights_shape = (n_ctx, FF_PAD, D)
    result = call(
        expert,
        jax.ShapeDtypeStruct((tall_rows, LANES), BF16),
        scratch=[
            pltpu.VMEM((n_ctx, depth, D), BF16),
            pltpu.VMEM(weights_shape, BF16),
            pltpu.VMEM(weights_shape, BF16),
            pltpu.VMEM(weights_shape, BF16),
            pltpu.VMEM((values_width, D), BF16),
            pltpu.VMEM((tall_rows, LANES), F32),
            pltpu.VMEM((short_rows, LANES), F32),
            pltpu.VMEM((rows, values_width), BF16),
            pltpu.VMEM((rows, D), F32),
            pltpu.SemaphoreType.DMA((4,)),
        ],
        flops=4 << 30,
        moved=16 << 20,
        in_specs=[vmem()] * 3 + [pl.BlockSpec(memory_space=pl.ANY)],
    )(
        residual_rows.reshape(tall_rows, LANES),
        values_rows.reshape(short_rows, LANES),
        norm_gain.reshape(1, D),
        packed_all,
    )
    returned = lax.all_to_all(
        result.reshape(n_exp, tall_rows // n_exp, LANES), "exp", split_axis=0, concat_axis=0, tiled=True
    )

    attended = call(
        home,
        jax.ShapeDtypeStruct((tokens, D), BF16),
        scratch=[
            pltpu.VMEM((n_ctx, depth, D), BF16),
            pltpu.VMEM((values_width, D), BF16),
            pltpu.SemaphoreType.DMA,
        ],
        flops=2 * tokens * D * values_width,
        moved=6 << 20,
        in_specs=[vmem()] * 2 + [pl.BlockSpec(memory_space=pl.ANY)],
    )(residual[0], values, packed_all)
    layer_out = call(
        combine,
        jax.ShapeDtypeStruct((tokens, D), BF16),
        scratch=[pltpu.VMEM((tall_rows, LANES), F32)],
        flops=4 * rows * tokens * D,
        moved=3 << 20,
    )(slots, route_weights[0], attended, returned.reshape(tall_rows, LANES))
    return layer_out[None]


def solution(mesh):
    return jax.shard_map(
        body,
        mesh=mesh,
        in_specs=(
            P("exp", "ctx", None),
            P("exp", "ctx", None),
            P("exp", "ctx", None),
            P(),
            P(),
            P(None, "ctx"),
            P(),
            P("exp", None, "ctx"),
            P("exp", None, "ctx"),
            P("exp", "ctx", None),
            P("exp", "ctx", None),
            P("exp", "ctx", None),
        ),
        out_specs=P("exp", "ctx", None),
        check_vma=False,
    )
```

```python
import jax
import jax.numpy as jnp
from jax import lax
from jax.experimental import pallas as pl
from jax.experimental.pallas import tpu as pltpu
from jax.sharding import PartitionSpec as P

D = 2048
HEADS = 8
NOPE = 128
ROPE = 64
QK = NOPE + ROPE
VHEAD = 128
LATENT = 512
FF_DEV = 44
FF_PAD = 48
CAP = 9
LANES = 128
F32 = jnp.float32
BF16 = jnp.bfloat16
NT = (((1,), (1,)), ((), ()))
TN = (((0,), (0,)), ((), ()))


def call(kernel, out_shape, scratch=(), flops=0, moved=0, in_specs=None, limit=16):
    options = {} if in_specs is None else {"in_specs": in_specs}
    return pl.pallas_call(
        kernel,
        out_shape=out_shape,
        scratch_shapes=list(scratch),
        compiler_params=pltpu.CompilerParams(vmem_limit_bytes=limit << 20),
        cost_estimate=pl.CostEstimate(flops=flops, bytes_accessed=moved, transcendentals=0),
        **options,
    )


def vmem():
    return pl.BlockSpec(memory_space=pltpu.VMEM)


def slot_matrix(slots, k, rows):
    return lax.broadcasted_iota(jnp.int32, (rows, slots.shape[1]), 0) == slots[k : k + 1, :]


def both_choices(slots, rows):
    return (slot_matrix(slots, 0, rows) | slot_matrix(slots, 1, rows)).astype(BF16)


def put_column(j, column, blocks):
    count = blocks.shape[0]
    parts = blocks.shape[1] // CAP
    blocks[:, 8 * j : 8 * j + 8, :] = column[: 8 * count].reshape(count, 8, LANES)
    blocks[:, 8 * parts + j, :] = column[8 * count :]


def put_pair(j, chunk, extra, out_ref):
    count = extra.shape[0]
    columns = [chunk[:, :LANES], chunk[:, LANES:]]
    whole = jnp.concatenate([c[: 8 * count].reshape(count, 8, LANES) for c in columns], axis=1)
    out_ref[:, 8 * j : 8 * j + 16, :] = whole.astype(BF16)
    for n, c in enumerate(columns):
        extra[:, j + n, :] = c[8 * count :]


def take_column(j, blocks):
    count = blocks.shape[0]
    parts = blocks.shape[1] // CAP
    whole = blocks[:, 8 * j : 8 * j + 8, :].reshape(8 * count, LANES)
    return jnp.concatenate([whole, blocks[:, 8 * parts + j, :]], axis=0)


def load_blocks(source_ref, blocks):
    blocks[...] = source_ref[...].astype(F32).reshape(blocks.shape)


def store_blocks(blocks, out_ref):
    out_ref[...] = blocks[...].reshape(out_ref.shape).astype(BF16)


def fill_rows(matrix, source_ref, blocks, out_ref):
    for j in range(0, source_ref.shape[1] // LANES, 2):
        chunk = jnp.dot(matrix, source_ref[:, j * LANES : (j + 2) * LANES], preferred_element_type=F32)
        put_column(j, chunk[:, :LANES], blocks)
        put_column(j + 1, chunk[:, LANES:], blocks)
    store_blocks(blocks, out_ref)


def begin(
    core_ref, projection_ref, gate_ref, up_ref, down_ref, routes_ref, residual_ref,
    packed_ref, out_ref, slots_ref, extra,
):
    columns = projection_ref[...].T
    part = columns.shape[0] // 4
    depth = columns.shape[1]
    columns = jnp.where(core_ref[0] == 0, columns[: 2 * part], columns[2 * part :])
    packed_ref[:part, :depth] = columns[:part]
    packed_ref[:part, depth:] = columns[part:]
    zeros = jnp.zeros((FF_PAD - FF_DEV, D), BF16)
    for n, ref in enumerate((gate_ref, up_ref, down_ref)):
        packed_ref[part + n * FF_PAD : part + (n + 1) * FF_PAD, :] = jnp.concatenate([ref[...], zeros], axis=0)
    tokens = routes_ref.shape[1]
    count = extra.shape[0]
    rows = count * CAP
    expert = lax.broadcasted_iota(jnp.int32, (LANES, tokens), 0)
    first = (expert == routes_ref[0:1, :]).astype(F32)
    second = (expert == routes_ref[1:2, :]).astype(F32)
    row = lax.broadcasted_iota(jnp.int32, (tokens, tokens), 0)
    column = lax.broadcasted_iota(jnp.int32, (tokens, tokens), 1)
    before = (row < column).astype(BF16)
    count_first = jnp.dot(first.astype(BF16), before, preferred_element_type=F32)
    count_second = jnp.dot(second.astype(BF16), before, preferred_element_type=F32)
    count_second = count_second + jnp.sum(first, axis=1, keepdims=True)
    place_first = jnp.sum(count_first * first, axis=0, keepdims=True).astype(jnp.int32)
    place_second = jnp.sum(count_second * second, axis=0, keepdims=True).astype(jnp.int32)
    chosen = routes_ref[...]
    place = jnp.concatenate([place_first, place_second], axis=0)
    slots = jnp.where(place < 8, chosen * 8 + place, 8 * count + chosen)
    slots_ref[...] = slots
    matrix = both_choices(slots, rows)
    for j in range(0, D // LANES, 2):
        chunk = jnp.dot(matrix, residual_ref[:, j * LANES : (j + 2) * LANES], preferred_element_type=F32)
        put_pair(j, chunk, extra, out_ref)
    out_ref[:, 8 * D // LANES :, :] = extra[...].astype(BF16)


def absorb(queries_ref, key_up_ref, out_ref):
    tokens = queries_ref.shape[0]
    for h in range(HEADS):
        query = queries_ref[:, h * QK : (h + 1) * QK]
        keys = key_up_ref[:, h * NOPE : (h + 1) * NOPE]
        out_ref[h * tokens : (h + 1) * tokens, :LATENT] = lax.dot_general(
            query[:, :NOPE], keys, NT, preferred_element_type=F32
        ).astype(BF16)
        out_ref[h * tokens : (h + 1) * tokens, LATENT:] = query[:, NOPE:]


def attend(key_at_ref, place_ref, absorbed_ref, keys, state, g):
    group = absorbed_ref.shape[0] // (HEADS // 2)
    tokens = group // 2
    query_at = lax.broadcasted_iota(jnp.int32, (group, 1), 0) % tokens + place_ref[0] * tokens
    score = jnp.dot(absorbed_ref[g * group : (g + 1) * group, :], keys[...], preferred_element_type=F32)
    score = jnp.where(key_at_ref[...] <= query_at, score * QK ** (-0.5), -1e30)
    highest = jnp.max(score, axis=1, keepdims=True)
    if state is not None:
        highest = jnp.maximum(highest, state[1])
    expo = jnp.exp(score - highest)
    denominator = jnp.sum(expo, axis=1, keepdims=True)
    summed = lax.dot_general(expo.astype(BF16), keys[:LATENT, :], NT, preferred_element_type=F32)
    if state is not None:
        factor = jnp.exp(state[1] - highest)
        summed = summed + state[0] * factor
        denominator = denominator + state[2] * factor
    return summed, highest, denominator


def lay_keys(refs, keys):
    at = 0
    for ref in refs:
        for b in range(ref.shape[0]):
            keys[:, at : at + ref.shape[2]] = ref[b]
            at += ref.shape[2]


def attend_first(place_ref, key_at_ref, near_ref, absorbed_ref, sum_ref, stats_ref, keys):
    lay_keys((near_ref,), keys)
    group = absorbed_ref.shape[0] // (HEADS // 2)
    for g in range(HEADS // 2):
        at = slice(g * group, (g + 1) * group)
        summed, highest, denominator = attend(key_at_ref, place_ref, absorbed_ref, keys, None, g)
        sum_ref[at, :] = summed
        stats_ref[at, 0:1] = highest
        stats_ref[at, 1:2] = denominator


def attend_more(
    place_ref, key_at_ref, up_ref, down_ref, absorbed_ref, sum_in_ref, stats_in_ref, sum_ref, stats_ref, keys
):
    lay_keys((up_ref, down_ref), keys)
    group = absorbed_ref.shape[0] // (HEADS // 2)
    for g in range(HEADS // 2):
        at = slice(g * group, (g + 1) * group)
        state = (sum_in_ref[at, :], stats_in_ref[at, 0:1], stats_in_ref[at, 1:2])
        summed, highest, denominator = attend(key_at_ref, place_ref, absorbed_ref, keys, state, g)
        sum_ref[at, :] = summed
        stats_ref[at, 0:1] = highest
        stats_ref[at, 1:2] = denominator


def attend_last(
    place_ref, slots_ref, key_at_ref, up_ref, down_ref, absorbed_ref, sum_in_ref, stats_in_ref,
    value_up_ref, values_ref, out_ref, keys, scratch,
):
    lay_keys((up_ref, down_ref), keys)
    tokens = values_ref.shape[0]
    group = 2 * tokens
    for g in range(HEADS // 2):
        at = slice(g * group, (g + 1) * group)
        state = (sum_in_ref[at, :], stats_in_ref[at, 0:1], stats_in_ref[at, 1:2])
        summed, highest, denominator = attend(key_at_ref, place_ref, absorbed_ref, keys, state, g)
        context = (summed / denominator).astype(BF16)
        for i in range(2):
            h = 2 * g + i
            values_ref[:, h * VHEAD : (h + 1) * VHEAD] = jnp.dot(
                context[i * tokens : (i + 1) * tokens],
                value_up_ref[:, h * VHEAD : (h + 1) * VHEAD],
                preferred_element_type=F32,
            ).astype(BF16)
    fill_rows(both_choices(slots_ref[...], scratch.shape[0] * CAP), values_ref, scratch, out_ref)


def unpack(blocks, parts, store):
    for j in range(parts):
        store[:, j * LANES : (j + 1) * LANES] = take_column(j, blocks).astype(BF16)


def start_all(pairs, sems):
    copies = [pltpu.make_async_copy(source, target, sems.at[n]) for n, (source, target) in enumerate(pairs)]
    for copy in copies:
        copy.start()
    return copies


def projection_pairs(core_ref, own_ref, other_ref, projection):
    part = projection.shape[1] // 4
    depth = projection.shape[2]
    pairs = []
    for n in range(4):
        ref, half = (own_ref, core_ref[0]) if n < 2 else (other_ref, 1 - core_ref[0])
        row = pl.multiple_of(half * (2 * part) + n % 2 * part, part)
        source = ref.at[:, 0:part, n % 2 * depth : (n % 2 + 1) * depth]
        pairs.append((source, projection.at[:, pl.ds(row, part), :]))
    return pairs


def take_part(packed_ref, part_ref, sem):
    copy = pltpu.make_async_copy(packed_ref.at[:, 0 : part_ref.shape[1], :], part_ref, sem)
    copy.start()
    copy.wait()


def project(values, projection):
    flat = projection[...].reshape(D, projection.shape[2])
    return lax.dot_general(values, flat, NT, preferred_element_type=F32)


def expert(
    core_ref, gain_ref, residual_ref, values_ref, packed_ref, other_ref, out_ref,
    residual_rows, value_rows, projection, gate, up, down, tall, short, residual, values, extra, sems,
):
    start = projection.shape[1] // 4
    pairs = [(values_ref, value_rows), (residual_ref, residual_rows)]
    pairs += projection_pairs(core_ref, packed_ref, other_ref, projection)
    pairs += [
        (packed_ref.at[:, start + n * FF_PAD : start + (n + 1) * FF_PAD, :], buffer)
        for n, buffer in enumerate((gate, up, down))
    ]
    copies = [pltpu.make_async_copy(source, target, sems.at[n]) for n, (source, target) in enumerate(pairs)]
    for copy in copies[:6]:
        copy.start()
    copies[0].wait()
    copies[6].start()
    load_blocks(value_rows, short)
    unpack(short, values.shape[1] // LANES, values)
    copies[1].wait()
    load_blocks(residual_rows, tall)
    unpack(tall, D // LANES, residual)
    for copy in copies[2:6]:
        copy.wait()
    copies[7].start()
    product = project(values[...], projection)
    attended = (residual[...].astype(F32) + product).astype(BF16).astype(F32)
    scale = lax.rsqrt(jnp.mean(attended * attended, axis=1, keepdims=True) + 1e-06)
    normed = (attended * scale * gain_ref[...]).astype(BF16)
    units = gate.shape[0] * gate.shape[1]
    copies[6].wait()
    copies[8].start()
    gate_proj = lax.dot_general(normed, gate[...].reshape(units, D), NT, preferred_element_type=F32)
    copies[7].wait()
    up_proj = lax.dot_general(normed, up[...].reshape(units, D), NT, preferred_element_type=F32)
    activation = (gate_proj / (1.0 + jnp.exp(-gate_proj)) * up_proj).astype(BF16)
    copies[8].wait()
    for j in range(0, D // LANES, 2):
        columns = down[:, :, j * LANES : (j + 2) * LANES].reshape(units, 2 * LANES)
        put_pair(j, jnp.dot(activation, columns, preferred_element_type=F32), extra, out_ref)
    out_ref[:, 8 * D // LANES :, :] = extra[...].astype(BF16)


def home(core_ref, residual_ref, values_ref, packed_ref, other_ref, out_ref, projection, sems):
    for copy in start_all(projection_pairs(core_ref, packed_ref, other_ref, projection), sems):
        copy.wait()
    projected = project(values_ref[...], projection)
    out_ref[...] = (residual_ref[...].astype(F32) + projected).astype(BF16)


def combine(slots_ref, weights_ref, attended_ref, rows_ref, out_ref, blocks, attended, result, sems):
    copy = pltpu.make_async_copy(attended_ref, attended, sems.at[0])
    copy.start()
    slots = slots_ref[...]
    tokens = slots.shape[1]
    rows = blocks.shape[0] * CAP
    first = slot_matrix(slots, 0, rows).astype(BF16)
    second = slot_matrix(slots, 1, rows).astype(BF16)
    same = lax.broadcasted_iota(jnp.int32, (tokens, tokens), 0) == lax.broadcasted_iota(
        jnp.int32, (tokens, tokens), 1
    )
    weights = [jnp.sum(jnp.where(same, weights_ref[k : k + 1, :], 0.0), axis=1, keepdims=True) for k in range(2)]
    load_blocks(rows_ref, blocks)
    copy.wait()
    copies = []
    for j in range(0, D // LANES, 2):
        pair = jnp.concatenate([take_column(j, blocks), take_column(j + 1, blocks)], axis=1).astype(BF16)
        picked_first = lax.dot_general(first, pair, TN, preferred_element_type=F32)
        picked_second = lax.dot_general(second, pair, TN, preferred_element_type=F32)
        mixed = picked_first * weights[0] + picked_second * weights[1]
        at = slice(j * LANES, (j + 2) * LANES)
        result[:, at] = (attended[:, at].astype(F32) + mixed).astype(BF16)
        if j % 4 == 2:
            at = slice((j - 2) * LANES, (j + 2) * LANES)
            copies.append(pltpu.make_async_copy(result.at[:, at], out_ref.at[:, at], sems.at[1 + j // 4]))
            copies[-1].start()
    for copy in copies:
        copy.wait()


def body(
    residual, queries, latent, key_up, value_up, out_proj, norm_gain,
    w_gate, w_up, w_down, routes, route_weights,
):
    tokens = residual.shape[1]
    n_ctx = lax.axis_size("ctx")
    n_exp = lax.axis_size("exp")
    rows = n_exp * CAP
    values_width = HEADS * VHEAD
    tall_rows = rows * D // LANES
    short_rows = rows * values_width // LANES
    tall = pltpu.VMEM((n_exp, tall_rows // n_exp, LANES), F32)
    extra = pltpu.VMEM((n_exp, D // LANES, LANES), F32)
    short = pltpu.VMEM((n_exp, short_rows // n_exp, LANES), F32)

    smem = pl.BlockSpec(memory_space=pltpu.SMEM)
    core = (lax.axis_index("exp").astype(jnp.int32) % 2).reshape(1)
    part = out_proj.shape[1] // 4
    packed, residual_out, slots = call(
        begin,
        [
            jax.ShapeDtypeStruct((part + 3 * FF_PAD, D), BF16),
            jax.ShapeDtypeStruct((n_exp, tall_rows // n_exp, LANES), BF16),
            jax.ShapeDtypeStruct((2, tokens), jnp.int32),
        ],
        scratch=[extra],
        flops=2 * rows * tokens * D,
        moved=3 << 20,
        in_specs=[smem] + [vmem()] * 6,
        limit=60,
    )(core, out_proj, w_gate[0].T, w_up[0].T, w_down[0], routes[0].T, residual[0])
    packed_all = lax.all_gather(packed, "ctx")
    residual_rows = lax.all_to_all(residual_out, "exp", split_axis=0, concat_axis=0, tiled=True)

    block, residual_out = lax.optimization_barrier((latent[0].T, residual_out))
    side = 4

    def send(array, columns):
        pairs = [(x * side + y, to * side + y) for x, to in columns for y in range(side)]
        return lax.ppermute(array, "ctx", pairs)

    rows_of_y = [[x * side + y for y in range(side)] for x in range(side)]
    near = lax.all_gather(block, "ctx", axis_index_groups=rows_of_y)
    up = send(near, [(0, 1), (1, 2), (2, 3)])
    down = send(near, [(0, 3), (1, 0)])
    far_up = send(up[:2], [(1, 2), (2, 3)])
    far_down = send(down[2:], [(0, 3), (3, 2)])
    here = lax.axis_index("ctx").astype(jnp.int32)
    owner = [(here // side + dx + side) % side * side + y for dx in (0, -1, 1, -2) for y in range(side)]
    key_at = (jnp.stack(owner)[:, None] * tokens + jnp.arange(tokens, dtype=jnp.int32)[None, :]).reshape(1, -1)
    third = side * tokens

    absorbed = call(
        absorb,
        jax.ShapeDtypeStruct((HEADS * tokens, LATENT + ROPE), BF16),
        flops=2 * tokens * HEADS * NOPE * LATENT,
        moved=3 << 20,
    )(queries[0], key_up)
    place = here.reshape(1)
    width = LATENT + ROPE
    state = [
        jax.ShapeDtypeStruct((HEADS * tokens, LATENT), F32),
        jax.ShapeDtypeStruct((HEADS * tokens, 2), F32),
    ]
    summed, stats = call(
        attend_first,
        state,
        scratch=[pltpu.VMEM((width, third), BF16)],
        flops=1 << 30,
        moved=6 << 20,
        in_specs=[smem] + [vmem()] * 3,
    )(place, key_at[:, :third], near, absorbed)
    summed, stats = call(
        attend_more,
        state,
        scratch=[pltpu.VMEM((width, 2 * third), BF16)],
        flops=2 << 30,
        moved=6 << 20,
        in_specs=[smem] + [vmem()] * 6,
        limit=24,
    )(place, key_at[:, third : 3 * third], up, down, absorbed, summed, stats)
    values, values_out = call(
        attend_last,
        [
            jax.ShapeDtypeStruct((tokens, values_width), BF16),
            jax.ShapeDtypeStruct((short_rows, LANES), BF16),
        ],
        scratch=[pltpu.VMEM((width, third), BF16), short],
        flops=1 << 30,
        moved=6 << 20,
        in_specs=[smem] + [vmem()] * 8,
        limit=20,
    )(place, slots, key_at[:, 3 * third :], far_up, far_down, absorbed, summed, stats, value_up)
    values_out, residual_rows = lax.optimization_barrier((values_out, residual_rows))
    values_rows = lax.all_to_all(
        values_out.reshape(n_exp, short_rows // n_exp, LANES), "exp", split_axis=0, concat_axis=0, tiled=True
    )

    any_space = pl.BlockSpec(memory_space=pl.ANY)
    projection = pltpu.VMEM((n_ctx, 4 * part, values_width), BF16)
    own_part = call(
        take_part,
        jax.ShapeDtypeStruct((n_ctx, part, D), BF16),
        scratch=[pltpu.SemaphoreType.DMA],
        moved=4 << 20,
        in_specs=[any_space],
        limit=60,
    )(packed_all)
    other_part = lax.ppermute(own_part, "exp", [(e, e + 1 - 2 * (e % 2)) for e in range(n_exp)])
    result = call(
        expert,
        jax.ShapeDtypeStruct((n_exp, tall_rows // n_exp, LANES), BF16),
        scratch=[pltpu.VMEM((tall_rows, LANES), BF16), pltpu.VMEM((short_rows, LANES), BF16), projection]
        + [pltpu.VMEM((n_ctx, FF_PAD, D), BF16)] * 3
        + [tall, short, pltpu.VMEM((rows, D), BF16), pltpu.VMEM((rows, values_width), BF16)]
        + [extra, pltpu.SemaphoreType.DMA((9,))],
        flops=4 << 30,
        moved=16 << 20,
        in_specs=[smem, vmem()] + [any_space] * 4,
        limit=60,
    )(
        core,
        norm_gain.reshape(1, D),
        residual_rows.reshape(tall_rows, LANES),
        values_rows.reshape(short_rows, LANES),
        packed_all,
        other_part,
    )
    returned = lax.all_to_all(
        result, "exp", split_axis=0, concat_axis=0, tiled=True
    )

    attended = call(
        home,
        jax.ShapeDtypeStruct((tokens, D), BF16),
        scratch=[projection, pltpu.SemaphoreType.DMA((4,))],
        flops=2 * tokens * D * values_width,
        moved=6 << 20,
        in_specs=[smem, vmem(), vmem(), any_space, any_space],
        limit=60,
    )(core, residual[0], values, packed_all, other_part)
    layer_out = pl.pallas_call(
        combine,
        out_shape=jax.ShapeDtypeStruct((tokens, D), BF16),
        in_specs=[vmem(), vmem(), any_space, vmem()],
        out_specs=any_space,
        scratch_shapes=[tall, pltpu.VMEM((tokens, D), BF16), pltpu.VMEM((tokens, D), BF16)]
        + [pltpu.SemaphoreType.DMA((5,))],
        input_output_aliases={2: 0},
        compiler_params=pltpu.CompilerParams(vmem_limit_bytes=16 << 20),
        cost_estimate=pl.CostEstimate(flops=4 * rows * tokens * D, bytes_accessed=3 << 20, transcendentals=0),
    )(slots, route_weights[0].T, attended, returned.reshape(tall_rows, LANES))
    return layer_out[None]


def solution(mesh):
    return jax.shard_map(
        body,
        mesh=mesh,
        in_specs=(
            P("exp", "ctx", None),
            P("exp", "ctx", None),
            P("exp", "ctx", None),
            P(),
            P(),
            P(None, "ctx"),
            P(),
            P("exp", None, "ctx"),
            P("exp", None, "ctx"),
            P("exp", "ctx", None),
            P("exp", "ctx", None),
            P("exp", "ctx", None),
        ),
        out_specs=P("exp", "ctx", None),
        check_vma=False,
    )
```

```python
import jax
import jax.numpy as jnp
from jax import lax
from jax.experimental import pallas as pl
from jax.experimental.pallas import tpu as pltpu
from jax.sharding import PartitionSpec as P

D = 2048
HEADS = 8
NOPE = 128
ROPE = 64
QK = NOPE + ROPE
VHEAD = 128
LATENT = 512
FF_DEV = 44
FF_PAD = 48
CAP = 9
LANES = 128
F32 = jnp.float32
BF16 = jnp.bfloat16
NT = (((1,), (1,)), ((), ()))
TN = (((0,), (0,)), ((), ()))


def call(kernel, out_shape, scratch=(), flops=0, moved=0, in_specs=None, limit=16):
    options = {} if in_specs is None else {"in_specs": in_specs}
    return pl.pallas_call(
        kernel,
        out_shape=out_shape,
        scratch_shapes=list(scratch),
        compiler_params=pltpu.CompilerParams(vmem_limit_bytes=limit << 20),
        cost_estimate=pl.CostEstimate(flops=flops, bytes_accessed=moved, transcendentals=0),
        **options,
    )


def vmem():
    return pl.BlockSpec(memory_space=pltpu.VMEM)


def slot_matrix(slots, k, rows):
    return lax.broadcasted_iota(jnp.int32, (rows, slots.shape[1]), 0) == slots[k : k + 1, :]


def both_choices(slots, rows):
    return (slot_matrix(slots, 0, rows) | slot_matrix(slots, 1, rows)).astype(BF16)


def put_column(j, column, blocks):
    count = blocks.shape[0]
    parts = blocks.shape[1] // CAP
    blocks[:, 8 * j : 8 * j + 8, :] = column[: 8 * count].reshape(count, 8, LANES)
    blocks[:, 8 * parts + j, :] = column[8 * count :]


def put_pair(j, chunk, extra, out_ref):
    count = extra.shape[0]
    columns = [chunk[:, :LANES], chunk[:, LANES:]]
    whole = jnp.concatenate([c[: 8 * count].reshape(count, 8, LANES) for c in columns], axis=1)
    out_ref[:, 8 * j : 8 * j + 16, :] = whole.astype(BF16)
    for n, c in enumerate(columns):
        extra[:, j + n, :] = c[8 * count :]


def take_column(j, blocks):
    count = blocks.shape[0]
    parts = blocks.shape[1] // CAP
    whole = blocks[:, 8 * j : 8 * j + 8, :].reshape(8 * count, LANES)
    return jnp.concatenate([whole, blocks[:, 8 * parts + j, :]], axis=0)


def load_blocks(source_ref, blocks):
    blocks[...] = source_ref[...].astype(F32).reshape(blocks.shape)


def store_blocks(blocks, out_ref):
    out_ref[...] = blocks[...].reshape(out_ref.shape).astype(BF16)


def fill_rows(matrix, source_ref, blocks, out_ref):
    for j in range(0, source_ref.shape[1] // LANES, 2):
        chunk = jnp.dot(matrix, source_ref[:, j * LANES : (j + 2) * LANES], preferred_element_type=F32)
        put_column(j, chunk[:, :LANES], blocks)
        put_column(j + 1, chunk[:, LANES:], blocks)
    store_blocks(blocks, out_ref)


def begin(
    core_ref, projection_ref, gate_ref, up_ref, down_ref, routes_ref, residual_ref,
    packed_ref, out_ref, slots_ref, extra,
):
    columns = projection_ref[...].T
    part = columns.shape[0] // 4
    depth = columns.shape[1]
    columns = jnp.where(core_ref[0] == 0, columns[: 2 * part], columns[2 * part :])
    packed_ref[:part, :depth] = columns[:part]
    packed_ref[:part, depth:] = columns[part:]
    zeros = jnp.zeros((FF_PAD - FF_DEV, D), BF16)
    for n, ref in enumerate((gate_ref, up_ref, down_ref)):
        packed_ref[part + n * FF_PAD : part + (n + 1) * FF_PAD, :] = jnp.concatenate([ref[...], zeros], axis=0)
    tokens = routes_ref.shape[1]
    count = extra.shape[0]
    rows = count * CAP
    expert = lax.broadcasted_iota(jnp.int32, (LANES, tokens), 0)
    first = (expert == routes_ref[0:1, :]).astype(F32)
    second = (expert == routes_ref[1:2, :]).astype(F32)
    row = lax.broadcasted_iota(jnp.int32, (tokens, tokens), 0)
    column = lax.broadcasted_iota(jnp.int32, (tokens, tokens), 1)
    before = (row < column).astype(BF16)
    count_first = jnp.dot(first.astype(BF16), before, preferred_element_type=F32)
    count_second = jnp.dot(second.astype(BF16), before, preferred_element_type=F32)
    count_second = count_second + jnp.sum(first, axis=1, keepdims=True)
    place_first = jnp.sum(count_first * first, axis=0, keepdims=True).astype(jnp.int32)
    place_second = jnp.sum(count_second * second, axis=0, keepdims=True).astype(jnp.int32)
    chosen = routes_ref[...]
    place = jnp.concatenate([place_first, place_second], axis=0)
    slots = jnp.where(place < 8, chosen * 8 + place, 8 * count + chosen)
    slots_ref[...] = slots
    matrix = both_choices(slots, rows)
    for j in range(0, D // LANES, 2):
        chunk = jnp.dot(matrix, residual_ref[:, j * LANES : (j + 2) * LANES], preferred_element_type=F32)
        put_pair(j, chunk, extra, out_ref)
    out_ref[:, 8 * D // LANES :, :] = extra[...].astype(BF16)


def absorb(queries_ref, key_up_ref, out_ref):
    tokens = queries_ref.shape[0]
    for h in range(HEADS):
        query = queries_ref[:, h * QK : (h + 1) * QK]
        keys = key_up_ref[:, h * NOPE : (h + 1) * NOPE]
        out_ref[h * tokens : (h + 1) * tokens, :LATENT] = lax.dot_general(
            query[:, :NOPE], keys, NT, preferred_element_type=F32
        ).astype(BF16)
        out_ref[h * tokens : (h + 1) * tokens, LATENT:] = query[:, NOPE:]


def attend(key_at_ref, place_ref, absorbed_ref, keys, state, g):
    group = absorbed_ref.shape[0] // (HEADS // 2)
    tokens = group // 2
    query_at = lax.broadcasted_iota(jnp.int32, (group, 1), 0) % tokens + place_ref[0] * tokens
    score = jnp.dot(absorbed_ref[g * group : (g + 1) * group, :], keys[...], preferred_element_type=F32)
    score = jnp.where(key_at_ref[...] <= query_at, score * QK ** (-0.5), -1e30)
    highest = jnp.max(score, axis=1, keepdims=True)
    if state is not None:
        highest = jnp.maximum(highest, state[1])
    expo = jnp.exp(score - highest)
    denominator = jnp.sum(expo, axis=1, keepdims=True)
    summed = lax.dot_general(expo.astype(BF16), keys[:LATENT, :], NT, preferred_element_type=F32)
    if state is not None:
        factor = jnp.exp(state[1] - highest)
        summed = summed + state[0] * factor
        denominator = denominator + state[2] * factor
    return summed, highest, denominator


def lay_keys(refs, keys):
    at = 0
    for ref in refs:
        for b in range(ref.shape[0]):
            keys[:, at : at + ref.shape[2]] = ref[b]
            at += ref.shape[2]


def attend_first(place_ref, key_at_ref, near_ref, absorbed_ref, sum_ref, stats_ref, keys):
    lay_keys((near_ref,), keys)
    group = absorbed_ref.shape[0] // (HEADS // 2)
    for g in range(HEADS // 2):
        at = slice(g * group, (g + 1) * group)
        summed, highest, denominator = attend(key_at_ref, place_ref, absorbed_ref, keys, None, g)
        sum_ref[at, :] = summed
        stats_ref[at, 0:1] = highest
        stats_ref[at, 1:2] = denominator


def attend_more(
    place_ref, key_at_ref, up_ref, down_ref, absorbed_ref, sum_in_ref, stats_in_ref, sum_ref, stats_ref, keys
):
    lay_keys((up_ref, down_ref), keys)
    group = absorbed_ref.shape[0] // (HEADS // 2)
    for g in range(HEADS // 2):
        at = slice(g * group, (g + 1) * group)
        state = (sum_in_ref[at, :], stats_in_ref[at, 0:1], stats_in_ref[at, 1:2])
        summed, highest, denominator = attend(key_at_ref, place_ref, absorbed_ref, keys, state, g)
        sum_ref[at, :] = summed
        stats_ref[at, 0:1] = highest
        stats_ref[at, 1:2] = denominator


def attend_last(
    place_ref, slots_ref, key_at_ref, up_ref, down_ref, absorbed_ref, sum_in_ref, stats_in_ref,
    value_up_ref, values_ref, out_ref, keys, scratch,
):
    lay_keys((up_ref, down_ref), keys)
    tokens = values_ref.shape[0]
    group = 2 * tokens
    for g in range(HEADS // 2):
        at = slice(g * group, (g + 1) * group)
        state = (sum_in_ref[at, :], stats_in_ref[at, 0:1], stats_in_ref[at, 1:2])
        summed, highest, denominator = attend(key_at_ref, place_ref, absorbed_ref, keys, state, g)
        context = (summed / denominator).astype(BF16)
        for i in range(2):
            h = 2 * g + i
            values_ref[:, h * VHEAD : (h + 1) * VHEAD] = jnp.dot(
                context[i * tokens : (i + 1) * tokens],
                value_up_ref[:, h * VHEAD : (h + 1) * VHEAD],
                preferred_element_type=F32,
            ).astype(BF16)
    fill_rows(both_choices(slots_ref[...], scratch.shape[0] * CAP), values_ref, scratch, out_ref)


def unpack(blocks, parts, store):
    for j in range(parts):
        store[:, j * LANES : (j + 1) * LANES] = take_column(j, blocks).astype(BF16)


def start_all(pairs, sems):
    copies = [pltpu.make_async_copy(source, target, sems.at[n]) for n, (source, target) in enumerate(pairs)]
    for copy in copies:
        copy.start()
    return copies


def projection_pairs(core_ref, own_ref, other_ref, projection):
    part = projection.shape[1] // 4
    depth = projection.shape[2]
    pairs = []
    for n in range(4):
        ref, half = (own_ref, core_ref[0]) if n < 2 else (other_ref, 1 - core_ref[0])
        row = pl.multiple_of(half * (2 * part) + n % 2 * part, part)
        source = ref.at[:, 0:part, n % 2 * depth : (n % 2 + 1) * depth]
        pairs.append((source, projection.at[:, pl.ds(row, part), :]))
    return pairs


def take_part(packed_ref, part_ref, sem):
    copy = pltpu.make_async_copy(packed_ref.at[:, 0 : part_ref.shape[1], :], part_ref, sem)
    copy.start()
    copy.wait()


def take_rest(
    packed_ref, residual_ref, values_ref, gate_ref, up_ref, down_ref, residual_out_ref, values_out_ref, tall, short, sems
):
    start = packed_ref.shape[1] - 3 * FF_PAD
    pairs = [
        (packed_ref.at[:, start + n * FF_PAD : start + (n + 1) * FF_PAD, :], ref)
        for n, ref in enumerate((gate_ref, up_ref, down_ref))
    ]
    copies = start_all(pairs, sems)
    load_blocks(residual_ref, tall)
    unpack(tall, D // LANES, residual_out_ref)
    load_blocks(values_ref, short)
    unpack(short, values_out_ref.shape[1] // LANES, values_out_ref)
    for copy in copies:
        copy.wait()


def project(values, projection):
    flat = projection[...].reshape(D, projection.shape[2])
    return lax.dot_general(values, flat, NT, preferred_element_type=F32)


def expert(
    core_ref, gain_ref, residual_ref, values_ref, own_ref, other_ref, gate_ref, up_ref, down_ref, out_ref,
    projection, extra,
):
    part = own_ref.shape[1]
    depth = projection.shape[2]
    for ref, half in ((own_ref, core_ref[0]), (other_ref, 1 - core_ref[0])):
        for n in range(2):
            row = pl.multiple_of(half * (2 * part) + n * part, part)
            projection[:, pl.ds(row, part), :] = ref[:, :, n * depth : (n + 1) * depth]
    product = project(values_ref[...], projection)
    attended = (residual_ref[...].astype(F32) + product).astype(BF16).astype(F32)
    scale = lax.rsqrt(jnp.mean(attended * attended, axis=1, keepdims=True) + 1e-06)
    normed = (attended * scale * gain_ref[...]).astype(BF16)
    units = gate_ref.shape[0] * FF_PAD
    gate_proj = lax.dot_general(normed, gate_ref[...].reshape(units, D), NT, preferred_element_type=F32)
    up_proj = lax.dot_general(normed, up_ref[...].reshape(units, D), NT, preferred_element_type=F32)
    activation = (gate_proj / (1.0 + jnp.exp(-gate_proj)) * up_proj).astype(BF16)
    for j in range(0, D // LANES, 2):
        columns = down_ref[:, :, j * LANES : (j + 2) * LANES].reshape(units, 2 * LANES)
        put_pair(j, jnp.dot(activation, columns, preferred_element_type=F32), extra, out_ref)
    out_ref[:, 8 * D // LANES :, :] = extra[...].astype(BF16)


def home(core_ref, residual_ref, values_ref, packed_ref, other_ref, out_ref, projection, sems):
    for copy in start_all(projection_pairs(core_ref, packed_ref, other_ref, projection), sems):
        copy.wait()
    projected = project(values_ref[...], projection)
    out_ref[...] = (residual_ref[...].astype(F32) + projected).astype(BF16)


def combine(slots_ref, weights_ref, attended_ref, rows_ref, out_ref, blocks, attended, result, sems):
    copy = pltpu.make_async_copy(attended_ref, attended, sems.at[0])
    copy.start()
    slots = slots_ref[...]
    tokens = slots.shape[1]
    rows = blocks.shape[0] * CAP
    first = slot_matrix(slots, 0, rows).astype(BF16)
    second = slot_matrix(slots, 1, rows).astype(BF16)
    same = lax.broadcasted_iota(jnp.int32, (tokens, tokens), 0) == lax.broadcasted_iota(
        jnp.int32, (tokens, tokens), 1
    )
    weights = [jnp.sum(jnp.where(same, weights_ref[k : k + 1, :], 0.0), axis=1, keepdims=True) for k in range(2)]
    load_blocks(rows_ref, blocks)
    copy.wait()
    copies = []
    for j in range(0, D // LANES, 2):
        pair = jnp.concatenate([take_column(j, blocks), take_column(j + 1, blocks)], axis=1).astype(BF16)
        picked_first = lax.dot_general(first, pair, TN, preferred_element_type=F32)
        picked_second = lax.dot_general(second, pair, TN, preferred_element_type=F32)
        mixed = picked_first * weights[0] + picked_second * weights[1]
        at = slice(j * LANES, (j + 2) * LANES)
        result[:, at] = (attended[:, at].astype(F32) + mixed).astype(BF16)
        if j % 4 == 2:
            at = slice((j - 2) * LANES, (j + 2) * LANES)
            copies.append(pltpu.make_async_copy(result.at[:, at], out_ref.at[:, at], sems.at[1 + j // 4]))
            copies[-1].start()
    for copy in copies:
        copy.wait()


def body(
    residual, queries, latent, key_up, value_up, out_proj, norm_gain,
    w_gate, w_up, w_down, routes, route_weights,
):
    tokens = residual.shape[1]
    n_ctx = lax.axis_size("ctx")
    n_exp = lax.axis_size("exp")
    rows = n_exp * CAP
    values_width = HEADS * VHEAD
    tall_rows = rows * D // LANES
    short_rows = rows * values_width // LANES
    tall = pltpu.VMEM((n_exp, tall_rows // n_exp, LANES), F32)
    extra = pltpu.VMEM((n_exp, D // LANES, LANES), F32)
    short = pltpu.VMEM((n_exp, short_rows // n_exp, LANES), F32)

    smem = pl.BlockSpec(memory_space=pltpu.SMEM)
    core = (lax.axis_index("exp").astype(jnp.int32) % 2).reshape(1)
    part = out_proj.shape[1] // 4
    packed, residual_out, slots = call(
        begin,
        [
            jax.ShapeDtypeStruct((part + 3 * FF_PAD, D), BF16),
            jax.ShapeDtypeStruct((n_exp, tall_rows // n_exp, LANES), BF16),
            jax.ShapeDtypeStruct((2, tokens), jnp.int32),
        ],
        scratch=[extra],
        flops=2 * rows * tokens * D,
        moved=3 << 20,
        in_specs=[smem] + [vmem()] * 6,
        limit=60,
    )(core, out_proj, w_gate[0].T, w_up[0].T, w_down[0], routes[0].T, residual[0])
    packed_all = lax.all_gather(packed, "ctx")
    residual_rows = lax.all_to_all(residual_out, "exp", split_axis=0, concat_axis=0, tiled=True)

    block, residual_out = lax.optimization_barrier((latent[0].T, residual_out))
    side = 4

    def send(array, columns):
        pairs = [(x * side + y, to * side + y) for x, to in columns for y in range(side)]
        return lax.ppermute(array, "ctx", pairs)

    rows_of_y = [[x * side + y for y in range(side)] for x in range(side)]
    near = lax.all_gather(block, "ctx", axis_index_groups=rows_of_y)
    up = send(near, [(0, 1), (1, 2), (2, 3)])
    down = send(near, [(0, 3), (1, 0)])
    far_up = send(up[:2], [(1, 2), (2, 3)])
    far_down = send(down[2:], [(0, 3), (3, 2)])
    here = lax.axis_index("ctx").astype(jnp.int32)
    owner = [(here // side + dx + side) % side * side + y for dx in (0, -1, 1, -2) for y in range(side)]
    key_at = (jnp.stack(owner)[:, None] * tokens + jnp.arange(tokens, dtype=jnp.int32)[None, :]).reshape(1, -1)
    third = side * tokens

    absorbed = call(
        absorb,
        jax.ShapeDtypeStruct((HEADS * tokens, LATENT + ROPE), BF16),
        flops=2 * tokens * HEADS * NOPE * LATENT,
        moved=3 << 20,
    )(queries[0], key_up)
    place = here.reshape(1)
    width = LATENT + ROPE
    state = [
        jax.ShapeDtypeStruct((HEADS * tokens, LATENT), F32),
        jax.ShapeDtypeStruct((HEADS * tokens, 2), F32),
    ]
    summed, stats = call(
        attend_first,
        state,
        scratch=[pltpu.VMEM((width, third), BF16)],
        flops=1 << 30,
        moved=6 << 20,
        in_specs=[smem] + [vmem()] * 3,
    )(place, key_at[:, :third], near, absorbed)
    summed, stats = call(
        attend_more,
        state,
        scratch=[pltpu.VMEM((width, 2 * third), BF16)],
        flops=2 << 30,
        moved=6 << 20,
        in_specs=[smem] + [vmem()] * 6,
        limit=24,
    )(place, key_at[:, third : 3 * third], up, down, absorbed, summed, stats)
    values, values_out = call(
        attend_last,
        [
            jax.ShapeDtypeStruct((tokens, values_width), BF16),
            jax.ShapeDtypeStruct((short_rows, LANES), BF16),
        ],
        scratch=[pltpu.VMEM((width, third), BF16), short],
        flops=1 << 30,
        moved=6 << 20,
        in_specs=[smem] + [vmem()] * 8,
        limit=20,
    )(place, slots, key_at[:, 3 * third :], far_up, far_down, absorbed, summed, stats, value_up)
    values_out, residual_rows = lax.optimization_barrier((values_out, residual_rows))
    values_rows = lax.all_to_all(
        values_out.reshape(n_exp, short_rows // n_exp, LANES), "exp", split_axis=0, concat_axis=0, tiled=True
    )

    any_space = pl.BlockSpec(memory_space=pl.ANY)
    projection = pltpu.VMEM((n_ctx, 4 * part, values_width), BF16)
    own_part = call(
        take_part,
        jax.ShapeDtypeStruct((n_ctx, part, D), BF16),
        scratch=[pltpu.SemaphoreType.DMA],
        moved=4 << 20,
        in_specs=[any_space],
        limit=60,
    )(packed_all)
    other_part = lax.ppermute(own_part, "exp", [(e, e + 1 - 2 * (e % 2)) for e in range(n_exp)])
    gate, up, down, residual_kept, values_kept = call(
        take_rest,
        [pltpu.VMEM((n_ctx, FF_PAD, D), BF16)] * 3
        + [pltpu.VMEM((rows, D), BF16), pltpu.VMEM((rows, values_width), BF16)],
        scratch=[tall, short, pltpu.SemaphoreType.DMA((3,))],
        moved=16 << 20,
        in_specs=[any_space, vmem(), vmem()],
        limit=42,
    )(packed_all, residual_rows.reshape(tall_rows, LANES), values_rows.reshape(short_rows, LANES))
    result = call(
        expert,
        jax.ShapeDtypeStruct((n_exp, tall_rows // n_exp, LANES), BF16),
        scratch=[projection, extra],
        flops=4 << 30,
        moved=8 << 20,
        in_specs=[smem] + [vmem()] * 8,
        limit=24,
    )(core, norm_gain.reshape(1, D), residual_kept, values_kept, own_part, other_part, gate, up, down)
    returned = lax.all_to_all(
        result, "exp", split_axis=0, concat_axis=0, tiled=True
    )

    attended = call(
        home,
        jax.ShapeDtypeStruct((tokens, D), BF16),
        scratch=[projection, pltpu.SemaphoreType.DMA((4,))],
        flops=2 * tokens * D * values_width,
        moved=6 << 20,
        in_specs=[smem, vmem(), vmem(), any_space, any_space],
        limit=60,
    )(core, residual[0], values, packed_all, other_part)
    layer_out = pl.pallas_call(
        combine,
        out_shape=jax.ShapeDtypeStruct((tokens, D), BF16),
        in_specs=[vmem(), vmem(), any_space, vmem()],
        out_specs=any_space,
        scratch_shapes=[tall, pltpu.VMEM((tokens, D), BF16), pltpu.VMEM((tokens, D), BF16)]
        + [pltpu.SemaphoreType.DMA((5,))],
        input_output_aliases={2: 0},
        compiler_params=pltpu.CompilerParams(vmem_limit_bytes=16 << 20),
        cost_estimate=pl.CostEstimate(flops=4 * rows * tokens * D, bytes_accessed=3 << 20, transcendentals=0),
    )(slots, route_weights[0].T, attended, returned.reshape(tall_rows, LANES))
    return layer_out[None]


def solution(mesh):
    return jax.shard_map(
        body,
        mesh=mesh,
        in_specs=(
            P("exp", "ctx", None),
            P("exp", "ctx", None),
            P("exp", "ctx", None),
            P(),
            P(),
            P(None, "ctx"),
            P(),
            P("exp", None, "ctx"),
            P("exp", None, "ctx"),
            P("exp", "ctx", None),
            P("exp", "ctx", None),
            P("exp", "ctx", None),
        ),
        out_specs=P("exp", "ctx", None),
        check_vma=False,
    )
```

```python
import jax
import jax.numpy as jnp
from jax import lax
from jax.experimental import pallas as pl
from jax.experimental.pallas import tpu as pltpu
from jax.sharding import PartitionSpec as P

D = 2048
HEADS = 8
NOPE = 128
ROPE = 64
QK = NOPE + ROPE
VHEAD = 128
LATENT = 512
FF_DEV = 44
FF_PAD = 48
CAP = 9
LANES = 128
F32 = jnp.float32
BF16 = jnp.bfloat16
NT = (((1,), (1,)), ((), ()))
TN = (((0,), (0,)), ((), ()))


def call(kernel, out_shape, scratch=(), flops=0, moved=0, in_specs=None, limit=16):
    options = {} if in_specs is None else {"in_specs": in_specs}
    return pl.pallas_call(
        kernel,
        out_shape=out_shape,
        scratch_shapes=list(scratch),
        compiler_params=pltpu.CompilerParams(vmem_limit_bytes=limit << 20),
        cost_estimate=pl.CostEstimate(flops=flops, bytes_accessed=moved, transcendentals=0),
        **options,
    )


def vmem():
    return pl.BlockSpec(memory_space=pltpu.VMEM)


def slot_matrix(slots, k, rows):
    return lax.broadcasted_iota(jnp.int32, (rows, slots.shape[1]), 0) == slots[k : k + 1, :]


def both_choices(slots, rows):
    return (slot_matrix(slots, 0, rows) | slot_matrix(slots, 1, rows)).astype(BF16)


def put_column(j, column, blocks):
    count = blocks.shape[0]
    parts = blocks.shape[1] // CAP
    blocks[:, 8 * j : 8 * j + 8, :] = column[: 8 * count].reshape(count, 8, LANES)
    blocks[:, 8 * parts + j, :] = column[8 * count :]


def put_pair(j, chunk, extra, out_ref):
    count = extra.shape[0]
    columns = [chunk[:, :LANES], chunk[:, LANES:]]
    whole = jnp.concatenate([c[: 8 * count].reshape(count, 8, LANES) for c in columns], axis=1)
    out_ref[:, 8 * j : 8 * j + 16, :] = whole.astype(BF16)
    for n, c in enumerate(columns):
        extra[:, j + n, :] = c[8 * count :]


def take_column(j, blocks):
    count = blocks.shape[0]
    parts = blocks.shape[1] // CAP
    whole = blocks[:, 8 * j : 8 * j + 8, :].reshape(8 * count, LANES)
    return jnp.concatenate([whole, blocks[:, 8 * parts + j, :]], axis=0)


def load_blocks(source_ref, blocks):
    blocks[...] = source_ref[...].astype(F32).reshape(blocks.shape)


def store_blocks(blocks, out_ref):
    out_ref[...] = blocks[...].reshape(out_ref.shape).astype(BF16)


def fill_rows(matrix, source_ref, blocks, out_ref):
    for j in range(0, source_ref.shape[1] // LANES, 2):
        chunk = jnp.dot(matrix, source_ref[:, j * LANES : (j + 2) * LANES], preferred_element_type=F32)
        put_column(j, chunk[:, :LANES], blocks)
        put_column(j + 1, chunk[:, LANES:], blocks)
    store_blocks(blocks, out_ref)


def begin(
    core_ref, projection_ref, gate_ref, up_ref, down_ref, routes_ref, residual_ref,
    packed_ref, out_ref, slots_ref, extra,
):
    columns = projection_ref[...].T
    part = columns.shape[0] // 4
    depth = columns.shape[1]
    columns = jnp.where(core_ref[0] == 0, columns[: 2 * part], columns[2 * part :])
    packed_ref[:part, :depth] = columns[:part]
    packed_ref[:part, depth:] = columns[part:]
    zeros = jnp.zeros((FF_PAD - FF_DEV, D), BF16)
    for n, ref in enumerate((gate_ref, up_ref, down_ref)):
        packed_ref[part + n * FF_PAD : part + (n + 1) * FF_PAD, :] = jnp.concatenate([ref[...], zeros], axis=0)
    tokens = routes_ref.shape[1]
    count = extra.shape[0]
    rows = count * CAP
    expert = lax.broadcasted_iota(jnp.int32, (LANES, tokens), 0)
    first = (expert == routes_ref[0:1, :]).astype(F32)
    second = (expert == routes_ref[1:2, :]).astype(F32)
    row = lax.broadcasted_iota(jnp.int32, (tokens, tokens), 0)
    column = lax.broadcasted_iota(jnp.int32, (tokens, tokens), 1)
    before = (row < column).astype(BF16)
    count_first = jnp.dot(first.astype(BF16), before, preferred_element_type=F32)
    count_second = jnp.dot(second.astype(BF16), before, preferred_element_type=F32)
    count_second = count_second + jnp.sum(first, axis=1, keepdims=True)
    place_first = jnp.sum(count_first * first, axis=0, keepdims=True).astype(jnp.int32)
    place_second = jnp.sum(count_second * second, axis=0, keepdims=True).astype(jnp.int32)
    chosen = routes_ref[...]
    place = jnp.concatenate([place_first, place_second], axis=0)
    slots = jnp.where(place < 8, chosen * 8 + place, 8 * count + chosen)
    slots_ref[...] = slots
    matrix = both_choices(slots, rows)
    for j in range(0, D // LANES, 2):
        chunk = jnp.dot(matrix, residual_ref[:, j * LANES : (j + 2) * LANES], preferred_element_type=F32)
        put_pair(j, chunk, extra, out_ref)
    out_ref[:, 8 * D // LANES :, :] = extra[...].astype(BF16)


def absorb(queries_ref, key_up_ref, out_ref):
    tokens = queries_ref.shape[0]
    for h in range(HEADS):
        query = queries_ref[:, h * QK : (h + 1) * QK]
        keys = key_up_ref[:, h * NOPE : (h + 1) * NOPE]
        out_ref[h * tokens : (h + 1) * tokens, :LATENT] = lax.dot_general(
            query[:, :NOPE], keys, NT, preferred_element_type=F32
        ).astype(BF16)
        out_ref[h * tokens : (h + 1) * tokens, LATENT:] = query[:, NOPE:]


def attend(key_at_ref, place_ref, absorbed_ref, keys, state, g):
    group = absorbed_ref.shape[0] // (HEADS // 2)
    tokens = group // 2
    query_at = lax.broadcasted_iota(jnp.int32, (group, 1), 0) % tokens + place_ref[0] * tokens
    score = jnp.dot(absorbed_ref[g * group : (g + 1) * group, :], keys[...], preferred_element_type=F32)
    score = jnp.where(key_at_ref[...] <= query_at, score * QK ** (-0.5), -1e30)
    highest = jnp.max(score, axis=1, keepdims=True)
    if state is not None:
        highest = jnp.maximum(highest, state[1])
    expo = jnp.exp(score - highest)
    denominator = jnp.sum(expo, axis=1, keepdims=True)
    summed = lax.dot_general(expo.astype(BF16), keys[:LATENT, :], NT, preferred_element_type=F32)
    if state is not None:
        factor = jnp.exp(state[1] - highest)
        summed = summed + state[0] * factor
        denominator = denominator + state[2] * factor
    return summed, highest, denominator


def lay_keys(refs, keys):
    at = 0
    for ref in refs:
        for b in range(ref.shape[0]):
            keys[:, at : at + ref.shape[2]] = ref[b]
            at += ref.shape[2]


def attend_first(place_ref, key_at_ref, near_ref, absorbed_ref, sum_ref, stats_ref, keys):
    lay_keys((near_ref,), keys)
    group = absorbed_ref.shape[0] // (HEADS // 2)
    for g in range(HEADS // 2):
        at = slice(g * group, (g + 1) * group)
        summed, highest, denominator = attend(key_at_ref, place_ref, absorbed_ref, keys, None, g)
        sum_ref[at, :] = summed
        stats_ref[at, 0:1] = highest
        stats_ref[at, 1:2] = denominator


def attend_more(
    place_ref, key_at_ref, up_ref, down_ref, absorbed_ref, sum_in_ref, stats_in_ref, sum_ref, stats_ref, keys
):
    lay_keys((up_ref, down_ref), keys)
    group = absorbed_ref.shape[0] // (HEADS // 2)
    for g in range(HEADS // 2):
        at = slice(g * group, (g + 1) * group)
        state = (sum_in_ref[at, :], stats_in_ref[at, 0:1], stats_in_ref[at, 1:2])
        summed, highest, denominator = attend(key_at_ref, place_ref, absorbed_ref, keys, state, g)
        sum_ref[at, :] = summed
        stats_ref[at, 0:1] = highest
        stats_ref[at, 1:2] = denominator


def attend_last(
    place_ref, slots_ref, key_at_ref, up_ref, down_ref, absorbed_ref, sum_in_ref, stats_in_ref,
    value_up_ref, values_ref, out_ref, keys, scratch,
):
    lay_keys((up_ref, down_ref), keys)
    tokens = values_ref.shape[0]
    group = 2 * tokens
    for g in range(HEADS // 2):
        at = slice(g * group, (g + 1) * group)
        state = (sum_in_ref[at, :], stats_in_ref[at, 0:1], stats_in_ref[at, 1:2])
        summed, highest, denominator = attend(key_at_ref, place_ref, absorbed_ref, keys, state, g)
        context = (summed / denominator).astype(BF16)
        for i in range(2):
            h = 2 * g + i
            values_ref[:, h * VHEAD : (h + 1) * VHEAD] = jnp.dot(
                context[i * tokens : (i + 1) * tokens],
                value_up_ref[:, h * VHEAD : (h + 1) * VHEAD],
                preferred_element_type=F32,
            ).astype(BF16)
    fill_rows(both_choices(slots_ref[...], scratch.shape[0] * CAP), values_ref, scratch, out_ref)


def unpack(blocks, parts, store):
    for j in range(parts):
        store[:, j * LANES : (j + 1) * LANES] = take_column(j, blocks).astype(BF16)


def start_all(pairs, sems):
    copies = [pltpu.make_async_copy(source, target, sems.at[n]) for n, (source, target) in enumerate(pairs)]
    for copy in copies:
        copy.start()
    return copies


def projection_pairs(core_ref, own_ref, other_ref, projection):
    part = projection.shape[1] // 4
    depth = projection.shape[2]
    pairs = []
    for n in range(4):
        ref, half = (own_ref, core_ref[0]) if n < 2 else (other_ref, 1 - core_ref[0])
        row = pl.multiple_of(half * (2 * part) + n % 2 * part, part)
        source = ref.at[:, 0:part, n % 2 * depth : (n % 2 + 1) * depth]
        pairs.append((source, projection.at[:, pl.ds(row, part), :]))
    return pairs


def take_part(packed_ref, part_ref, sem):
    copy = pltpu.make_async_copy(packed_ref.at[:, 0 : part_ref.shape[1], :], part_ref, sem)
    copy.start()
    copy.wait()


def take_rest(
    packed_ref, residual_ref, values_ref, gate_ref, up_ref, residual_out_ref, values_out_ref, tall, short, sems
):
    start = packed_ref.shape[1] - 3 * FF_PAD
    pairs = [
        (packed_ref.at[:, start + n * FF_PAD : start + (n + 1) * FF_PAD, :], ref)
        for n, ref in enumerate((gate_ref, up_ref))
    ]
    copies = start_all(pairs, sems)
    load_blocks(residual_ref, tall)
    unpack(tall, D // LANES, residual_out_ref)
    load_blocks(values_ref, short)
    unpack(short, values_out_ref.shape[1] // LANES, values_out_ref)
    for copy in copies:
        copy.wait()


def project(values, projection):
    flat = projection[...].reshape(D, projection.shape[2])
    return lax.dot_general(values, flat, NT, preferred_element_type=F32)


def expert(
    core_ref, gain_ref, residual_ref, values_ref, own_ref, other_ref, gate_ref, up_ref, packed_ref, out_ref,
    projection, extra, down, sem,
):
    start = packed_ref.shape[1] - FF_PAD
    copy = pltpu.make_async_copy(packed_ref.at[:, start : start + FF_PAD, :], down, sem)
    copy.start()
    part = own_ref.shape[1]
    depth = projection.shape[2]
    for ref, half in ((own_ref, core_ref[0]), (other_ref, 1 - core_ref[0])):
        for n in range(2):
            row = pl.multiple_of(half * (2 * part) + n * part, part)
            projection[:, pl.ds(row, part), :] = ref[:, :, n * depth : (n + 1) * depth]
    product = project(values_ref[...], projection)
    attended = (residual_ref[...].astype(F32) + product).astype(BF16).astype(F32)
    scale = lax.rsqrt(jnp.mean(attended * attended, axis=1, keepdims=True) + 1e-06)
    normed = (attended * scale * gain_ref[...]).astype(BF16)
    units = gate_ref.shape[0] * FF_PAD
    gate_proj = lax.dot_general(normed, gate_ref[...].reshape(units, D), NT, preferred_element_type=F32)
    up_proj = lax.dot_general(normed, up_ref[...].reshape(units, D), NT, preferred_element_type=F32)
    activation = (gate_proj / (1.0 + jnp.exp(-gate_proj)) * up_proj).astype(BF16)
    copy.wait()
    for j in range(0, D // LANES, 2):
        columns = down[:, :, j * LANES : (j + 2) * LANES].reshape(units, 2 * LANES)
        put_pair(j, jnp.dot(activation, columns, preferred_element_type=F32), extra, out_ref)
    out_ref[:, 8 * D // LANES :, :] = extra[...].astype(BF16)


def home(core_ref, residual_ref, values_ref, packed_ref, other_ref, out_ref, projection, sems):
    for copy in start_all(projection_pairs(core_ref, packed_ref, other_ref, projection), sems):
        copy.wait()
    projected = project(values_ref[...], projection)
    out_ref[...] = (residual_ref[...].astype(F32) + projected).astype(BF16)


def combine(slots_ref, weights_ref, attended_ref, rows_ref, out_ref, blocks, attended, result, sems):
    copy = pltpu.make_async_copy(attended_ref, attended, sems.at[0])
    copy.start()
    slots = slots_ref[...]
    tokens = slots.shape[1]
    rows = blocks.shape[0] * CAP
    first = slot_matrix(slots, 0, rows).astype(BF16)
    second = slot_matrix(slots, 1, rows).astype(BF16)
    same = lax.broadcasted_iota(jnp.int32, (tokens, tokens), 0) == lax.broadcasted_iota(
        jnp.int32, (tokens, tokens), 1
    )
    weights = [jnp.sum(jnp.where(same, weights_ref[k : k + 1, :], 0.0), axis=1, keepdims=True) for k in range(2)]
    load_blocks(rows_ref, blocks)
    copy.wait()
    copies = []
    for j in range(0, D // LANES, 2):
        pair = jnp.concatenate([take_column(j, blocks), take_column(j + 1, blocks)], axis=1).astype(BF16)
        picked_first = lax.dot_general(first, pair, TN, preferred_element_type=F32)
        picked_second = lax.dot_general(second, pair, TN, preferred_element_type=F32)
        mixed = picked_first * weights[0] + picked_second * weights[1]
        at = slice(j * LANES, (j + 2) * LANES)
        result[:, at] = (attended[:, at].astype(F32) + mixed).astype(BF16)
        if j % 4 == 2:
            at = slice((j - 2) * LANES, (j + 2) * LANES)
            copies.append(pltpu.make_async_copy(result.at[:, at], out_ref.at[:, at], sems.at[1 + j // 4]))
            copies[-1].start()
    for copy in copies:
        copy.wait()


def body(
    residual, queries, latent, key_up, value_up, out_proj, norm_gain,
    w_gate, w_up, w_down, routes, route_weights,
):
    tokens = residual.shape[1]
    n_ctx = lax.axis_size("ctx")
    n_exp = lax.axis_size("exp")
    rows = n_exp * CAP
    values_width = HEADS * VHEAD
    tall_rows = rows * D // LANES
    short_rows = rows * values_width // LANES
    tall = pltpu.VMEM((n_exp, tall_rows // n_exp, LANES), F32)
    extra = pltpu.VMEM((n_exp, D // LANES, LANES), F32)
    short = pltpu.VMEM((n_exp, short_rows // n_exp, LANES), F32)

    smem = pl.BlockSpec(memory_space=pltpu.SMEM)
    core = (lax.axis_index("exp").astype(jnp.int32) % 2).reshape(1)
    part = out_proj.shape[1] // 4
    packed, residual_out, slots = call(
        begin,
        [
            jax.ShapeDtypeStruct((part + 3 * FF_PAD, D), BF16),
            jax.ShapeDtypeStruct((n_exp, tall_rows // n_exp, LANES), BF16),
            jax.ShapeDtypeStruct((2, tokens), jnp.int32),
        ],
        scratch=[extra],
        flops=2 * rows * tokens * D,
        moved=3 << 20,
        in_specs=[smem] + [vmem()] * 6,
        limit=60,
    )(core, out_proj, w_gate[0].T, w_up[0].T, w_down[0], routes[0].T, residual[0])
    packed_all = lax.all_gather(packed, "ctx")
    residual_rows = lax.all_to_all(residual_out, "exp", split_axis=0, concat_axis=0, tiled=True)

    block, residual_out = lax.optimization_barrier((latent[0].T, residual_out))
    side = 4

    def send(array, columns):
        pairs = [(x * side + y, to * side + y) for x, to in columns for y in range(side)]
        return lax.ppermute(array, "ctx", pairs)

    rows_of_y = [[x * side + y for y in range(side)] for x in range(side)]
    near = lax.all_gather(block, "ctx", axis_index_groups=rows_of_y)
    up = send(near, [(0, 1), (1, 2), (2, 3)])
    down = send(near, [(0, 3), (1, 0)])
    far_up = send(up[:2], [(1, 2), (2, 3)])
    far_down = send(down[2:], [(0, 3), (3, 2)])
    here = lax.axis_index("ctx").astype(jnp.int32)
    owner = [(here // side + dx + side) % side * side + y for dx in (0, -1, 1, -2) for y in range(side)]
    key_at = (jnp.stack(owner)[:, None] * tokens + jnp.arange(tokens, dtype=jnp.int32)[None, :]).reshape(1, -1)
    third = side * tokens

    absorbed = call(
        absorb,
        jax.ShapeDtypeStruct((HEADS * tokens, LATENT + ROPE), BF16),
        flops=2 * tokens * HEADS * NOPE * LATENT,
        moved=3 << 20,
    )(queries[0], key_up)
    place = here.reshape(1)
    width = LATENT + ROPE
    state = [
        jax.ShapeDtypeStruct((HEADS * tokens, LATENT), F32),
        jax.ShapeDtypeStruct((HEADS * tokens, 2), F32),
    ]
    summed, stats = call(
        attend_first,
        state,
        scratch=[pltpu.VMEM((width, third), BF16)],
        flops=1 << 30,
        moved=6 << 20,
        in_specs=[smem] + [vmem()] * 3,
    )(place, key_at[:, :third], near, absorbed)
    summed, stats = call(
        attend_more,
        state,
        scratch=[pltpu.VMEM((width, 2 * third), BF16)],
        flops=2 << 30,
        moved=6 << 20,
        in_specs=[smem] + [vmem()] * 6,
        limit=24,
    )(place, key_at[:, third : 3 * third], up, down, absorbed, summed, stats)
    values, values_out = call(
        attend_last,
        [
            jax.ShapeDtypeStruct((tokens, values_width), BF16),
            jax.ShapeDtypeStruct((short_rows, LANES), BF16),
        ],
        scratch=[pltpu.VMEM((width, third), BF16), short],
        flops=1 << 30,
        moved=6 << 20,
        in_specs=[smem] + [vmem()] * 8,
        limit=20,
    )(place, slots, key_at[:, 3 * third :], far_up, far_down, absorbed, summed, stats, value_up)
    values_out, residual_rows = lax.optimization_barrier((values_out, residual_rows))
    values_rows = lax.all_to_all(
        values_out.reshape(n_exp, short_rows // n_exp, LANES), "exp", split_axis=0, concat_axis=0, tiled=True
    )

    any_space = pl.BlockSpec(memory_space=pl.ANY)
    projection = pltpu.VMEM((n_ctx, 4 * part, values_width), BF16)
    own_part = call(
        take_part,
        jax.ShapeDtypeStruct((n_ctx, part, D), BF16),
        scratch=[pltpu.SemaphoreType.DMA],
        moved=4 << 20,
        in_specs=[any_space],
        limit=60,
    )(packed_all)
    other_part = lax.ppermute(own_part, "exp", [(e, e + 1 - 2 * (e % 2)) for e in range(n_exp)])
    gate, up, residual_kept, values_kept = call(
        take_rest,
        [pltpu.VMEM((n_ctx, FF_PAD, D), BF16)] * 2
        + [pltpu.VMEM((rows, D), BF16), pltpu.VMEM((rows, values_width), BF16)],
        scratch=[tall, short, pltpu.SemaphoreType.DMA((2,))],
        moved=16 << 20,
        in_specs=[any_space, vmem(), vmem()],
        limit=46,
    )(packed_all, residual_rows.reshape(tall_rows, LANES), values_rows.reshape(short_rows, LANES))
    result = call(
        expert,
        jax.ShapeDtypeStruct((n_exp, tall_rows // n_exp, LANES), BF16),
        scratch=[projection, extra, pltpu.VMEM((n_ctx, FF_PAD, D), BF16), pltpu.SemaphoreType.DMA],
        flops=4 << 30,
        moved=8 << 20,
        in_specs=[smem] + [vmem()] * 7 + [any_space],
        limit=46,
    )(core, norm_gain.reshape(1, D), residual_kept, values_kept, own_part, other_part, gate, up, packed_all)
    returned = lax.all_to_all(
        result, "exp", split_axis=0, concat_axis=0, tiled=True
    )

    attended = call(
        home,
        jax.ShapeDtypeStruct((tokens, D), BF16),
        scratch=[projection, pltpu.SemaphoreType.DMA((4,))],
        flops=2 * tokens * D * values_width,
        moved=6 << 20,
        in_specs=[smem, vmem(), vmem(), any_space, any_space],
        limit=60,
    )(core, residual[0], values, packed_all, other_part)
    layer_out = pl.pallas_call(
        combine,
        out_shape=jax.ShapeDtypeStruct((tokens, D), BF16),
        in_specs=[vmem(), vmem(), any_space, vmem()],
        out_specs=any_space,
        scratch_shapes=[tall, pltpu.VMEM((tokens, D), BF16), pltpu.VMEM((tokens, D), BF16)]
        + [pltpu.SemaphoreType.DMA((5,))],
        input_output_aliases={2: 0},
        compiler_params=pltpu.CompilerParams(vmem_limit_bytes=16 << 20),
        cost_estimate=pl.CostEstimate(flops=4 * rows * tokens * D, bytes_accessed=3 << 20, transcendentals=0),
    )(slots, route_weights[0].T, attended, returned.reshape(tall_rows, LANES))
    return layer_out[None]


def solution(mesh):
    return jax.shard_map(
        body,
        mesh=mesh,
        in_specs=(
            P("exp", "ctx", None),
            P("exp", "ctx", None),
            P("exp", "ctx", None),
            P(),
            P(),
            P(None, "ctx"),
            P(),
            P("exp", None, "ctx"),
            P("exp", None, "ctx"),
            P("exp", "ctx", None),
            P("exp", "ctx", None),
            P("exp", "ctx", None),
        ),
        out_specs=P("exp", "ctx", None),
        check_vma=False,
    )
```
